256 devices in a mesh: grp: 8 (over z_lo, core), cut: 8 (over z_hi, x), st: 4 (over y).
Axes of the slice: x: 4, y: 4, z: 8 (z_hi: 2, z_lo: 4; z = z_hi * 4 + z_lo), core: 2. Of those that a mesh axis runs over, the one named last changes fastest.
Arguments:
- coefficients: bfloat16 [8192, 2048], P(('grp', 'cut')), may hold values from -0.125 to 0.125
- intercepts: bfloat16 [8192], P(('grp', 'cut')), may hold values from -6 to 6
- states: bfloat16 [65536, 2048], P(('grp', 'st')), may hold values from -6 to 6
- old_values: float32 [65536], P(('grp', 'st')), may hold values from 3.5 to 6.5
Outputs:
- new_values: float32 [65536], P(('grp', 'st'))
- cut_gaps: float32 [8192], P(('grp', 'cut'))
The draws below stay inside these ranges and needn't reach their ends.
All inputs are finite; a program needn't handle non-finite values.
Results may differ from the reference program's by a relative error of at most 0.0003.
Values may be sent and summed in bfloat16 or wider, within the bound.
No kernel may reach another device: no remote copies, remote signals or barrier semaphores. Data moves between devices by JAX's collectives and lax.ppermute only.
A program may use at most 64 MiB of HBM per device.

```python
import jax
import jax.numpy as jnp
from jax import lax

S = 2048
CUT_DEV = 128
NCUT = 8192
NST = 65536


def block_levels(key, shape, cuts, least, high):
    factor_of, own = 1.0, jax.random.fold_in(key, 6)
    for dim, blocks in cuts:
        heights = jnp.exp(jax.random.uniform(jax.random.fold_in(own, dim), (blocks,), jnp.float32, least / len(cuts), high / len(cuts)))
        factor_of = factor_of * jnp.repeat(heights, shape[dim] // blocks).reshape([-1 if axis == dim else 1 for axis in range(len(shape))])
    return factor_of


def bell_draw(own_key, extent, scale, bound, split=(), kind=jnp.bfloat16):
    drawn = jax.random.normal(own_key, extent, jnp.float32) * scale
    if len(split) > 0:
        drawn = block_levels(own_key, extent, split, -0.22, 0.18) * drawn
    return jnp.clip(drawn, min=-bound, max=bound).astype(kind)


def setup_inputs(seed: int = 0) -> dict:
    seeds = jax.random.split(jax.random.key(seed), 5)
    coefficients = bell_draw(seeds[0], (NCUT, S), S ** -0.5, 0.125, ((0, 64),))
    intercepts = bell_draw(seeds[1], (NCUT,), 1.0, 6.0, ((0, 64),))
    states = bell_draw(seeds[2], (NST, S), 1.0, 6.0, ((0, 32),))
    old_values = jnp.clip(3.5 + 3.0 * jax.random.uniform(seeds[3], (NST,), jnp.float32) ** block_levels(seeds[3], (NST,), ((0, 32),), -0.2, 0.2), 3.5, 6.5)
    return {"coefficients": coefficients, "intercepts": intercepts, "states": states, "old_values": old_values}


def reference(coefficients, intercepts, states, old_values):
    blocks = NCUT // CUT_DEV
    slopes = coefficients.reshape(blocks, CUT_DEV, S)
    offsets = intercepts.reshape(blocks, CUT_DEV)

    def visit(top_value, pieces):
        slope_rows, offset_rows = pieces
        scores = lax.dot_general(slope_rows, states, (((1,), (1,)), ((), ())), preferred_element_type=jnp.float32)
        scores = scores + offset_rows.astype(jnp.float32)[:, None]
        top_value = jnp.maximum(top_value, jnp.max(scores, axis=0))
        lifted = jnp.max(scores - old_values[None, :], axis=1)
        return top_value, lifted

    start_value = jnp.full((NST,), -jnp.inf, dtype=jnp.float32)
    top_value, lifts = lax.scan(visit, start_value, (slopes, offsets))
    new_values = jnp.maximum(old_values, top_value)
    return new_values, lifts.reshape(NCUT)
```

```python
import functools

import jax
import jax.numpy as jnp
from jax import lax
from jax.experimental import pallas as pl
from jax.experimental.pallas import tpu as pltpu
from jax.sharding import PartitionSpec as P

AXES = ("grp", "cut", "st")
NX, NY, NZ, NC = 4, 4, 8, 2


def position(x, y, z, c):
    z_hi, z_lo = divmod(z % NZ, 4)
    return (((z_lo * NC + c % NC) * 8) + z_hi * NX + x % NX) * NY + y % NY


def routes(move):
    pairs = []
    for x in range(NX):
        for y in range(NY):
            for z in range(NZ):
                for c in range(NC):
                    pairs.append((position(x, y, z, c), position(*move(x, y, z, c))))
    return pairs


def send(block, move):
    return lax.ppermute(block, AXES, routes(move))


def over_core(x, y, z, c):
    return x, y, z, 1 - c


def up(x, y, z, c):
    return x, y, z + 1, c


def down(x, y, z, c):
    return x, y, z - 1, c


def two_out(x, y, z, c):
    return x, y, z - 2 if c == 0 else z + 2, c


def two_back(x, y, z, c):
    return x, y, z + 2 if c == 0 else z - 2, c


def far(x, y, z, c):
    return x, y, z + 4, c


def score_body(tile, tiles, mine, other, bias, old, prev, states, top, lift, slopes, best, offset):
    rows = mine.shape[0]
    step = pl.program_id(0)

    @pl.when(step == 0)
    def _():
        slopes[:rows, :] = mine[...]
        slopes[rows:, :] = other[...]
        for part in range(2):
            spread = jnp.broadcast_to(bias[part : part + 1, :], (128, rows))
            offset[part * rows : (part + 1) * rows, :] = spread.T
        best[...] = jnp.full(best.shape, -jnp.inf, jnp.float32)

    scores = lax.dot_general(
        slopes[...], states[...], (((1,), (1,)), ((), ())), preferred_element_type=jnp.float32
    )
    lifted = scores - old[...]
    most = best[...]
    for lane in range(0, tile, 128):
        most = jnp.maximum(most, lifted[:, lane : lane + 128])
    best[...] = most
    wide = offset[...]
    valued = jnp.concatenate(
        [scores[:, lane : lane + 128] + wide for lane in range(0, tile, 128)], axis=1
    )
    top[...] = jnp.maximum(prev[...], jnp.max(valued, axis=0, keepdims=True))

    @pl.when(step == tiles - 1)
    def _():
        turned = jnp.max(best[...].T, axis=0, keepdims=True)
        for part in range(2):
            lift[part : part + 1, :] = turned[:, part * rows : (part + 1) * rows] + bias[part : part + 1, :]


def score(mine, other, bias, old, prev, states, tile=1024):
    rows, depth = mine.shape
    count = states.shape[0]
    tiles = count // tile
    whole = lambda shape: pl.BlockSpec(shape, lambda i: (0, 0))
    along = pl.BlockSpec((1, tile), lambda i: (0, i))
    return pl.pallas_call(
        functools.partial(score_body, tile, tiles),
        grid=(tiles,),
        in_specs=[
            whole((rows, depth)),
            whole((rows, depth)),
            whole((2, rows)),
            along,
            along,
            pl.BlockSpec((tile, depth), lambda i: (i, 0)),
        ],
        out_specs=[along, whole((2, rows))],
        out_shape=[
            jax.ShapeDtypeStruct((1, count), jnp.float32),
            jax.ShapeDtypeStruct((2, rows), jnp.float32),
        ],
        scratch_shapes=[
            pltpu.VMEM((2 * rows, depth), jnp.bfloat16),
            pltpu.VMEM((2 * rows, 128), jnp.float32),
            pltpu.VMEM((2 * rows, 128), jnp.float32),
        ],
        compiler_params=pltpu.CompilerParams(vmem_limit_bytes=24 << 20),
        cost_estimate=pl.CostEstimate(
            flops=4 * rows * depth * count, bytes_accessed=2 * (count + 2 * rows) * depth, transcendentals=0
        ),
    )(mine, other, bias, old, prev, states)


def body(coefficients, intercepts, states, old_values):
    old = old_values[None, :]
    offsets = intercepts.astype(jnp.float32)[None, :]

    two = send(coefficients, two_out)
    lower = send(coefficients, up)
    upper = send(coefficients, down)
    peer = send(coefficients, over_core)
    offsets_two = send(offsets, two_out)
    pair = jnp.concatenate([offsets, send(offsets, over_core)], axis=0)
    pair_lower = send(pair, up)
    pair_upper = send(pair, down)
    pair_two = jnp.concatenate([offsets_two, send(offsets_two, over_core)], axis=0)

    top, lift_own = score(coefficients, peer, pair, old, old, states)
    top, lift_lower = score(lower, send(lower, over_core), pair_lower, old, top, states)
    top, lift_upper = score(upper, send(upper, over_core), pair_upper, old, top, states)
    top, lift_two = score(two, send(two, over_core), pair_two, old, top, states)

    for_x = [send(top, lambda x, y, z, c, d=d: (x ^ d, y, z, c)) for d in (1, 2, 3)]
    top = functools.reduce(jnp.maximum, for_x, top)
    new_values = jnp.maximum(top, send(top, far))

    lifts = jnp.concatenate([lift_own, lift_lower, lift_upper, lift_two], axis=0).reshape(4, 2, -1)
    lifts = jnp.maximum(lifts[:, 0], send(lifts[:, 1], over_core))
    for_y = [send(lifts, lambda x, y, z, c, d=d: (x, y ^ d, z, c)) for d in (1, 2, 3)]
    lifts = functools.reduce(jnp.maximum, for_y, lifts)
    back = [send(lifts[1:2], down), send(lifts[2:3], up), send(lifts[3:4], two_back)]
    cut_gaps = functools.reduce(jnp.maximum, back, lifts[0:1])
    return new_values[0], cut_gaps[0]


def solution(mesh):
    placed = (P(("grp", "cut"), None), P(("grp", "cut")), P(("grp", "st"), None), P(("grp", "st")))
    return jax.shard_map(
        body,
        mesh=mesh,
        in_specs=placed,
        out_specs=(P(("grp", "st")), P(("grp", "cut"))),
        check_vma=False,
    )
```

```python
import functools

import jax
import jax.numpy as jnp
from jax import lax
from jax.experimental import pallas as pl
from jax.experimental.pallas import tpu as pltpu
from jax.sharding import PartitionSpec as P

AXES = ("grp", "cut", "st")
NX, NY, NZ, NC = 4, 4, 8, 2
LANES = 128


def position(x, y, z, c):
    z_hi, z_lo = divmod(z % NZ, 4)
    return (((z_lo * NC + c % NC) * 8) + z_hi * NX + x % NX) * NY + y % NY


def routes(move):
    pairs = []
    for x in range(NX):
        for y in range(NY):
            for z in range(NZ):
                for c in range(NC):
                    pairs.append((position(x, y, z, c), position(*move(x, y, z, c))))
    return pairs


def send(block, move):
    return lax.ppermute(block, AXES, routes(move))


def over_core(x, y, z, c):
    return x, y, z, 1 - c


def up(x, y, z, c):
    return x, y, z + 1, c


def down(x, y, z, c):
    return x, y, z - 1, c


def two_out(x, y, z, c):
    return x, y, z - 2 if c == 0 else z + 2, c


def two_back(x, y, z, c):
    return x, y, z + 2 if c == 0 else z - 2, c


def far(x, y, z, c):
    return x, y, z + 4, c


def over_x(d):
    return lambda x, y, z, c: (x ^ d, y, z, c)


def over_y(d):
    return lambda x, y, z, c: (x, y ^ d, z, c)


def score_body(tile, tiles, count, spots, y, old, prev, states, *refs):
    blocks, (top, mine, other, slopes, best, offset) = refs[:count], refs[count:]
    depth = states.shape[1]
    half = mine.shape[1]
    step = pl.program_id(0)

    @pl.when(step == 0)
    def _():
        for block, start, rows, base, mask in spots:
            place = base if mask is None else pl.multiple_of(base + (y[0] ^ mask) * rows, rows)
            slopes[pl.ds(place, rows), :] = blocks[block][start : start + rows, :depth]
            offset[pl.ds(place, rows), :] = blocks[block][start : start + rows, depth:].astype(jnp.float32)
        best[...] = jnp.full(best.shape, -jnp.inf, jnp.float32)

    scores = lax.dot_general(
        slopes[...], states[...], (((1,), (1,)), ((), ())), preferred_element_type=jnp.float32
    )
    lifted = scores - old[...]
    most = best[...]
    for lane in range(0, tile, LANES):
        most = jnp.maximum(most, lifted[:, lane : lane + LANES])
    best[...] = most
    wide = offset[...]
    valued = jnp.concatenate(
        [scores[:, lane : lane + LANES] + wide for lane in range(0, tile, LANES)], axis=1
    )
    top[...] = jnp.maximum(prev[...], jnp.max(valued, axis=0, keepdims=True))

    @pl.when(step == tiles - 1)
    def _():
        lift = jnp.max((best[...] + offset[...]).T, axis=0, keepdims=True)
        mine[...] = lift[:, :half]
        other[...] = lift[:, half:]


def score(spots, blocks, y, old, prev, states, tile=1024):
    count, depth = states.shape
    cuts = sum(spot[2] for spot in spots)
    tiles = count // tile
    whole = lambda shape: pl.BlockSpec(shape, lambda i, y: (0, 0))
    along = pl.BlockSpec((1, tile), lambda i, y: (0, i))
    lift = jax.ShapeDtypeStruct((1, cuts // 2), jnp.float32)
    return pl.pallas_call(
        functools.partial(score_body, tile, tiles, len(blocks), spots),
        grid_spec=pltpu.PrefetchScalarGridSpec(
            num_scalar_prefetch=1,
            grid=(tiles,),
            in_specs=[along, along, pl.BlockSpec((tile, depth), lambda i, y: (i, 0))]
            + [whole(block.shape) for block in blocks],
            out_specs=[along, whole(lift.shape), whole(lift.shape)],
            scratch_shapes=[
                pltpu.VMEM((cuts, depth), jnp.bfloat16),
                pltpu.VMEM((cuts, LANES), jnp.float32),
                pltpu.VMEM((cuts, LANES), jnp.float32),
            ],
        ),
        out_shape=[jax.ShapeDtypeStruct((1, count), jnp.float32), lift, lift],
        compiler_params=pltpu.CompilerParams(vmem_limit_bytes=24 << 20),
        cost_estimate=pl.CostEstimate(
            flops=2 * cuts * depth * count, bytes_accessed=2 * (count + cuts) * depth, transcendentals=0
        ),
    )(y, old, prev, states, *blocks)


def body(coefficients, intercepts, states, old_values):
    old = old_values[None, :]
    cuts = coefficients.shape[0]
    run = cuts // NY
    spread = jnp.broadcast_to(intercepts[:, None], (cuts, LANES))
    own = jnp.concatenate([coefficients, spread], axis=1)
    pair = ((0, 0, cuts, 0, None), (1, 0, cuts, cuts, None))

    y = lax.axis_index("st")
    quarter = lax.dynamic_slice_in_dim(own, y * run, run, 0)
    y = y[None]
    part = send(quarter, two_out)
    lower = send(own, up)
    upper = send(own, down)
    peer = send(own, over_core)
    parts = [part] + [send(part, over_y(d)) for d in (1, 2, 3)]
    top, own_mine, own_other = score(pair, [own, peer], y, old, old, states)
    lower, upper, top = lax.optimization_barrier((lower, upper, top))
    two = jnp.concatenate(parts, axis=0)
    runs = tuple((b, k * run, run, b * cuts, k) for b in range(2) for k in range(NY))
    top, lower_mine, lower_other = score(pair, [lower, send(lower, over_core)], y, old, top, states)
    top, upper_mine, upper_other = score(pair, [upper, send(upper, over_core)], y, old, top, states)
    top, two_mine, two_other = score(runs, [two, send(two, over_core)], y, old, top, states)

    mine = jnp.concatenate([own_mine, lower_mine, upper_mine, two_mine], axis=0)
    other = jnp.concatenate([own_other, lower_other, upper_other, two_other], axis=0)
    swapped = send(other, over_core)
    for_x = [send(top, over_x(d)) for d in (1, 2, 3)]
    swapped, *for_x = lax.optimization_barrier((swapped, *for_x))
    lifts = jnp.maximum(mine, swapped)
    for_y = [send(lifts, over_y(d)) for d in (1, 2, 3)]
    top = functools.reduce(jnp.maximum, for_x, top)
    new_values = jnp.maximum(top, send(top, far))
    lifts = functools.reduce(jnp.maximum, for_y, lifts)
    back = [send(lifts[1:2], down), send(lifts[2:3], up), send(lifts[3:4], two_back)]
    cut_gaps = functools.reduce(jnp.maximum, back, lifts[0:1])
    return new_values[0], cut_gaps[0]


def solution(mesh):
    placed = (P(("grp", "cut"), None), P(("grp", "cut")), P(("grp", "st"), None), P(("grp", "st")))
    return jax.shard_map(
        body,
        mesh=mesh,
        in_specs=placed,
        out_specs=(P(("grp", "st")), P(("grp", "cut"))),
        check_vma=False,
    )
```

```python
import functools

import jax
import jax.numpy as jnp
from jax import lax
from jax.experimental import pallas as pl
from jax.experimental.pallas import tpu as pltpu
from jax.sharding import PartitionSpec as P

AXES = ("grp", "cut", "st")
NX, NY, NZ, NC = 4, 4, 8, 2
LANES = 128
PACK_FLOPS = 10**10


def position(x, y, z, c):
    z_hi, z_lo = divmod(z % NZ, 4)
    return (((z_lo * NC + c % NC) * 8) + z_hi * NX + x % NX) * NY + y % NY


def routes(move, cores):
    pairs = []
    for x in range(NX):
        for y in range(NY):
            for z in range(NZ):
                for c in cores:
                    pairs.append((position(x, y, z, c), position(*move(x, y, z, c))))
    return pairs


def send(block, move, cores=range(NC)):
    return lax.ppermute(block, AXES, routes(move, cores))


def over_core(x, y, z, c):
    return x, y, z, 1 - c


def up(x, y, z, c):
    return x, y, z + 1, c


def down(x, y, z, c):
    return x, y, z - 1, c


def two_out(x, y, z, c):
    return x, y, z - 2 if c == 0 else z + 2, c


def two_back(x, y, z, c):
    return x, y, z + 2 if c == 0 else z - 2, c


def far(x, y, z, c):
    return x, y, z + 4, c


def over_x(d):
    return lambda x, y, z, c: (x ^ d, y, z, c)


def over_y(d):
    return lambda x, y, z, c: (x, y ^ d, z, c)


def pack_body(y, coefficients, intercepts, own, quarter):
    cuts, depth = coefficients.shape
    run = quarter.shape[0]
    rows = pl.ds(pl.multiple_of(y[0] * run, run), run)
    own[:, :depth] = coefficients[...]
    wide = jnp.broadcast_to(intercepts[...].astype(jnp.float32), (LANES, cuts)).T
    own[:, depth:] = wide.astype(jnp.bfloat16)
    quarter[...] = own[rows, :]


def pack(y, coefficients, intercepts):
    cuts, depth = coefficients.shape
    whole = lambda shape: pl.BlockSpec(shape, lambda i, y: (0, 0))
    shapes = [(cuts, depth + LANES), (cuts // NY, depth + LANES)]
    return pl.pallas_call(
        pack_body,
        grid_spec=pltpu.PrefetchScalarGridSpec(
            num_scalar_prefetch=1,
            grid=(1,),
            in_specs=[whole((cuts, depth)), whole((1, cuts))],
            out_specs=[whole(shape) for shape in shapes],
        ),
        out_shape=[jax.ShapeDtypeStruct(shape, jnp.bfloat16) for shape in shapes],
        compiler_params=pltpu.CompilerParams(vmem_limit_bytes=24 << 20),
        cost_estimate=pl.CostEstimate(flops=PACK_FLOPS, bytes_accessed=4 * cuts * depth, transcendentals=0),
    )(y, coefficients, intercepts[None, :])


def score_body(tile, tiles, count, spots, y, old, prev, states, *refs):
    blocks, (top, mine, other, slopes, best, offset) = refs[:count], refs[count:]
    depth = states.shape[1]
    half = mine.shape[1]
    step = pl.program_id(0)

    @pl.when(step == 0)
    def _():
        for block, start, rows, base, mask in spots:
            place = base if mask is None else pl.multiple_of(base + (y[0] ^ mask) * rows, rows)
            slopes[pl.ds(place, rows), :] = blocks[block][start : start + rows, :depth]
            offset[pl.ds(place, rows), :] = blocks[block][start : start + rows, depth:].astype(jnp.float32)
        best[...] = jnp.full(best.shape, -jnp.inf, jnp.float32)

    scores = lax.dot_general(
        slopes[...], states[...], (((1,), (1,)), ((), ())), preferred_element_type=jnp.float32
    )
    lifted = scores - old[...]
    most = best[...]
    for lane in range(0, tile, LANES):
        most = jnp.maximum(most, lifted[:, lane : lane + LANES])
    best[...] = most
    wide = offset[...]
    valued = jnp.concatenate(
        [scores[:, lane : lane + LANES] + wide for lane in range(0, tile, LANES)], axis=1
    )
    top[...] = jnp.maximum(prev[...], jnp.max(valued, axis=0, keepdims=True))

    @pl.when(step == tiles - 1)
    def _():
        lift = jnp.max((best[...] + offset[...]).T, axis=0, keepdims=True)
        mine[...] = lift[:, :half]
        other[...] = lift[:, half:]


def score(spots, blocks, y, old, prev, states, tile=1024):
    count, depth = states.shape
    cuts = sum(spot[2] for spot in spots)
    tiles = count // tile
    whole = lambda shape: pl.BlockSpec(shape, lambda i, y: (0, 0))
    along = pl.BlockSpec((1, tile), lambda i, y: (0, i))
    lift = jax.ShapeDtypeStruct((1, cuts // 2), jnp.float32)
    return pl.pallas_call(
        functools.partial(score_body, tile, tiles, len(blocks), spots),
        grid_spec=pltpu.PrefetchScalarGridSpec(
            num_scalar_prefetch=1,
            grid=(tiles,),
            in_specs=[along, along, pl.BlockSpec((tile, depth), lambda i, y: (i, 0))]
            + [whole(block.shape) for block in blocks],
            out_specs=[along, whole(lift.shape), whole(lift.shape)],
            scratch_shapes=[
                pltpu.VMEM((cuts, depth), jnp.bfloat16),
                pltpu.VMEM((cuts, LANES), jnp.float32),
                pltpu.VMEM((cuts, LANES), jnp.float32),
            ],
        ),
        out_shape=[jax.ShapeDtypeStruct((1, count), jnp.float32), lift, lift],
        compiler_params=pltpu.CompilerParams(vmem_limit_bytes=24 << 20),
        cost_estimate=pl.CostEstimate(
            flops=2 * cuts * depth * count, bytes_accessed=2 * (count + cuts) * depth, transcendentals=0
        ),
    )(y, old, prev, states, *blocks)


def body(coefficients, intercepts, states, old_values):
    old = old_values[None, :]
    cuts = coefficients.shape[0]
    run = cuts // NY
    pair = ((0, 0, cuts, 0, None), (1, 0, cuts, cuts, None))
    runs = tuple((b, k * run, run, b * cuts, k) for b in range(2) for k in range(NY))
    y = lax.axis_index("st")[None]
    core = lax.axis_index("grp") % NC

    own, quarter = pack(y, coefficients, intercepts)
    part = send(quarter, two_out)
    lower = send(own, up)
    upper = send(own, down)
    peer = send(own, over_core)
    parts = [part] + [send(part, over_y(d)) for d in (1, 2, 3)]
    top, own_mine, own_other = score(pair, [own, peer], y, old, old, states)
    lower, upper, top = lax.optimization_barrier((lower, upper, top))
    two = jnp.concatenate(parts, axis=0)
    top, lower_mine, lower_other = score(pair, [lower, send(lower, over_core)], y, old, top, states)
    top, upper_mine, upper_other = score(pair, [upper, send(upper, over_core)], y, old, top, states)
    top, two_mine, two_other = score(runs, [two, send(two, over_core)], y, old, top, states)

    mine = jnp.concatenate([own_mine, lower_mine, upper_mine, two_mine], axis=1)
    other = jnp.concatenate([own_other, lower_other, upper_other, two_other], axis=1)
    swapped = send(jnp.concatenate([top, mine, other], axis=1), over_core)
    count, lanes = top.shape[1], mine.shape[1]
    tops = jnp.concatenate([top, swapped[:, :count]], axis=1)
    lifts = jnp.concatenate(
        [
            jnp.maximum(mine, swapped[:, count + lanes :]),
            jnp.maximum(other, swapped[:, count : count + lanes]),
        ],
        axis=0,
    )
    for_x = [send(tops, over_x(d), (0,)) for d in (1, 2, 3)]
    for_y = [send(lifts, over_y(d), (1,)) for d in (1, 2, 3)]
    tops = functools.reduce(jnp.maximum, for_x, tops)
    lifts = functools.reduce(jnp.maximum, for_y, lifts)
    split = [lifts[:, k * cuts : (k + 1) * cuts] for k in range(4)]
    back = [
        send(split[1], down, (1,)),
        send(split[2], up, (1,)),
        send(split[3][:1], lambda x, y, z, c: (x, y, z - 2, c), (1,)),
        send(split[3][1:], lambda x, y, z, c: (x, y, z + 2, c), (1,)),
    ]
    tops = jnp.maximum(tops, send(tops, far, (0,)))
    gaps = jnp.maximum(jnp.maximum(back[0], back[1]), jnp.concatenate(back[2:], axis=0))
    gaps = jnp.maximum(gaps, split[0])
    swapped = send(jnp.concatenate([tops[:, count:], gaps[1:]], axis=1), over_core)
    new_values = jnp.where(core == 0, tops[0, :count], swapped[0, :count])
    cut_gaps = jnp.where(core == 0, swapped[0, count:], gaps[0])
    return new_values, cut_gaps


def solution(mesh):
    placed = (P(("grp", "cut"), None), P(("grp", "cut")), P(("grp", "st"), None), P(("grp", "st")))
    return jax.shard_map(
        body,
        mesh=mesh,
        in_specs=placed,
        out_specs=(P(("grp", "st")), P(("grp", "cut"))),
        check_vma=False,
    )
```

```python
import functools

import jax
import jax.numpy as jnp
from jax import lax
from jax.experimental import pallas as pl
from jax.experimental.pallas import tpu as pltpu
from jax.sharding import PartitionSpec as P

AXES = ("grp", "cut", "st")
NX, NY, NZ, NC = 4, 4, 8, 2
LANES = 128
PACK_FLOPS = 10**10
PACK_VMEM = 24 << 20


def position(x, y, z, c):
    z_hi, z_lo = divmod(z % NZ, 4)
    return (((z_lo * NC + c % NC) * 8) + z_hi * NX + x % NX) * NY + y % NY


def routes(move):
    pairs = []
    for x in range(NX):
        for y in range(NY):
            for z in range(NZ):
                for c in range(NC):
                    pairs.append((position(x, y, z, c), position(*move(x, y, z, c))))
    return pairs


def send(block, move):
    return lax.ppermute(block, AXES, routes(move))


def over_core(x, y, z, c):
    return x, y, z, 1 - c


def toward(x, y, z, c):
    return x, y, z - 1 if c == 0 else z + 1, c


def against(x, y, z, c):
    return x, y, z + 1 if c == 0 else z - 1, c


def two_back(x, y, z, c):
    return x, y, z + 2 if c == 0 else z - 2, c


def far(x, y, z, c):
    return x, y, z + 4, c


def over_x(d):
    return lambda x, y, z, c: (x ^ d, y, z, c)


def over_y(d):
    return lambda x, y, z, c: (x, y ^ d, z, c)


def pack_body(coefficients, intercepts, own, slopes, row, arrived):
    depth = coefficients.shape[1]
    copies = [
        pltpu.make_async_copy(coefficients, slopes, arrived.at[0]),
        pltpu.make_async_copy(intercepts, row, arrived.at[1]),
    ]
    for copy in copies:
        copy.start()
    for copy in copies:
        copy.wait()
    own[:, :depth] = slopes[...]
    wide = jnp.broadcast_to(row[...].astype(jnp.float32), (LANES, row.shape[1])).T
    own[:, depth:] = wide.astype(jnp.bfloat16)


def pack(coefficients, intercepts):
    cuts, depth = coefficients.shape
    there = pl.BlockSpec(memory_space=pl.ANY)
    return pl.pallas_call(
        pack_body,
        in_specs=[there, there],
        out_specs=pl.BlockSpec(memory_space=pltpu.VMEM),
        out_shape=jax.ShapeDtypeStruct((cuts, depth + LANES), jnp.bfloat16),
        scratch_shapes=[
            pltpu.VMEM((cuts, depth), jnp.bfloat16),
            pltpu.VMEM((1, cuts), jnp.bfloat16),
            pltpu.SemaphoreType.DMA((2,)),
        ],
        compiler_params=pltpu.CompilerParams(vmem_limit_bytes=PACK_VMEM),
        cost_estimate=pl.CostEstimate(flops=PACK_FLOPS, bytes_accessed=4 * cuts * depth, transcendentals=0),
    )(coefficients, intercepts[None, :])


def score_body(tile, tiles, count, old, prev, states, *refs):
    blocks, (top, mine, other, slopes, best, offset) = refs[:count], refs[count:]
    depth = states.shape[1]
    half = mine.shape[1]
    step = pl.program_id(0)

    @pl.when(step == 0)
    def _():
        row = 0
        for block in blocks:
            rows = block.shape[0]
            slopes[row : row + rows, :] = block[:, :depth]
            offset[row : row + rows, :] = block[:, depth:].astype(jnp.float32)
            row += rows
        best[...] = jnp.full(best.shape, -jnp.inf, jnp.float32)

    scores = lax.dot_general(
        slopes[...], states[...], (((1,), (1,)), ((), ())), preferred_element_type=jnp.float32
    )
    lifted = scores - old[...]
    most = best[...]
    for lane in range(0, tile, LANES):
        most = jnp.maximum(most, lifted[:, lane : lane + LANES])
    best[...] = most
    wide = offset[...]
    valued = jnp.concatenate(
        [scores[:, lane : lane + LANES] + wide for lane in range(0, tile, LANES)], axis=1
    )
    top[...] = jnp.maximum(prev[...], jnp.max(valued, axis=0, keepdims=True))

    @pl.when(step == tiles - 1)
    def _():
        lift = jnp.max((best[...] + offset[...]).T, axis=0, keepdims=True)
        mine[...] = lift[:, :half]
        other[...] = lift[:, half:]


def score(blocks, old, prev, states, tile=1024):
    count, depth = states.shape
    cuts = sum(block.shape[0] for block in blocks)
    tiles = count // tile
    whole = lambda shape: pl.BlockSpec(shape, lambda i: (0, 0))
    along = pl.BlockSpec((1, tile), lambda i: (0, i))
    lift = jax.ShapeDtypeStruct((1, cuts // 2), jnp.float32)
    return pl.pallas_call(
        functools.partial(score_body, tile, tiles, len(blocks)),
        grid=(tiles,),
        in_specs=[along, along, pl.BlockSpec((tile, depth), lambda i: (i, 0))]
        + [whole(block.shape) for block in blocks],
        out_specs=[along, whole(lift.shape), whole(lift.shape)],
        out_shape=[jax.ShapeDtypeStruct((1, count), jnp.float32), lift, lift],
        scratch_shapes=[
            pltpu.VMEM((cuts, depth), jnp.bfloat16),
            pltpu.VMEM((cuts, LANES), jnp.float32),
            pltpu.VMEM((cuts, LANES), jnp.float32),
        ],
        compiler_params=pltpu.CompilerParams(vmem_limit_bytes=24 << 20),
        cost_estimate=pl.CostEstimate(
            flops=2 * cuts * depth * count, bytes_accessed=2 * (count + cuts) * depth, transcendentals=0
        ),
    )(old, prev, states, *blocks)


def body(coefficients, intercepts, states, old_values):
    old = old_values[None, :]
    fence = lax.optimization_barrier

    own = pack(coefficients, intercepts)
    near = send(own, toward)
    next_ = send(own, against)
    peer = send(own, over_core)
    top, own_mine, own_other = score([own, peer], old, old, states)
    near, next_, top = fence((near, next_, top))
    two = send(near, toward)
    top, near_mine, near_other = score([near, send(near, over_core)], old, top, states)
    top, next_mine, next_other = score([next_, send(next_, over_core)], old, top, states)

    mine = jnp.concatenate([own_mine, near_mine, next_mine], axis=0)
    other = jnp.concatenate([own_other, near_other, next_other], axis=0)
    lifts = jnp.maximum(mine, send(other, over_core))
    two, top, lifts = fence((two, top, lifts))
    back = [send(lifts[1:2], against), send(lifts[2:3], toward)]
    top, two_mine, two_other = score([two, send(two, over_core)], old, top, states)

    swapped = send(two_other, over_core)
    for_x = [send(top, over_x(d)) for d in (1, 2, 3)]
    held = functools.reduce(jnp.maximum, back, lifts[0:1])
    last = jnp.maximum(two_mine, swapped)
    lifts = jnp.concatenate([held, last], axis=0)
    for_y = [send(lifts, over_y(d)) for d in (1, 2, 3)]
    top = functools.reduce(jnp.maximum, for_x, top)
    lifts = functools.reduce(jnp.maximum, for_y, lifts)
    for_z = send(lifts[1:2], two_back)
    new_values = jnp.maximum(top, send(top, far))
    cut_gaps = jnp.maximum(lifts[0:1], for_z)
    return new_values[0], cut_gaps[0]


def solution(mesh):
    placed = (P(("grp", "cut"), None), P(("grp", "cut")), P(("grp", "st"), None), P(("grp", "st")))
    return jax.shard_map(
        body,
        mesh=mesh,
        in_specs=placed,
        out_specs=(P(("grp", "st")), P(("grp", "cut"))),
        check_vma=False,
    )
```

```python
import functools

import jax
import jax.numpy as jnp
from jax import lax
from jax.experimental import pallas as pl
from jax.experimental.pallas import tpu as pltpu
from jax.sharding import PartitionSpec as P

AXES = ("grp", "cut", "st")
NX, NY, NZ, NC = 4, 4, 8, 2
LANES = 128
PACK_FLOPS = 10**10
PACK_VMEM = 24 << 20


def position(x, y, z, c):
    z_hi, z_lo = divmod(z % NZ, 4)
    return (((z_lo * NC + c % NC) * 8) + z_hi * NX + x % NX) * NY + y % NY


def routes(move):
    pairs = []
    for x in range(NX):
        for y in range(NY):
            for z in range(NZ):
                for c in range(NC):
                    pairs.append((position(x, y, z, c), position(*move(x, y, z, c))))
    return pairs


def send(block, move):
    return lax.ppermute(block, AXES, routes(move))


def over_core(x, y, z, c):
    return x, y, z, 1 - c


def toward(x, y, z, c):
    return x, y, z - 1 if c == 0 else z + 1, c


def against(x, y, z, c):
    return x, y, z + 1 if c == 0 else z - 1, c


def two_back(x, y, z, c):
    return x, y, z + 2 if c == 0 else z - 2, c


def far(x, y, z, c):
    return x, y, z + 4, c


def over_x(d):
    return lambda x, y, z, c: (x ^ d, y, z, c)


def over_y(d):
    return lambda x, y, z, c: (x, y ^ d, z, c)


def pack_body(coefficients, intercepts, own, slopes, row, arrived):
    depth = coefficients.shape[1]
    copies = [
        pltpu.make_async_copy(coefficients, slopes, arrived.at[0]),
        pltpu.make_async_copy(intercepts, row, arrived.at[1]),
    ]
    for copy in copies:
        copy.start()
    for copy in copies:
        copy.wait()
    own[:, :depth] = slopes[...]
    wide = jnp.broadcast_to(row[...].astype(jnp.float32), (LANES, row.shape[1])).T
    own[:, depth:] = wide.astype(jnp.bfloat16)


def pack(coefficients, intercepts):
    cuts, depth = coefficients.shape
    there = pl.BlockSpec(memory_space=pl.ANY)
    return pl.pallas_call(
        pack_body,
        in_specs=[there, there],
        out_specs=pl.BlockSpec(memory_space=pltpu.VMEM),
        out_shape=jax.ShapeDtypeStruct((cuts, depth + LANES), jnp.bfloat16),
        scratch_shapes=[
            pltpu.VMEM((cuts, depth), jnp.bfloat16),
            pltpu.VMEM((1, cuts), jnp.bfloat16),
            pltpu.SemaphoreType.DMA((2,)),
        ],
        compiler_params=pltpu.CompilerParams(vmem_limit_bytes=PACK_VMEM),
        cost_estimate=pl.CostEstimate(flops=PACK_FLOPS, bytes_accessed=4 * cuts * depth, transcendentals=0),
    )(coefficients, intercepts[None, :])


def score_body(tile, tiles, count, old, prev, states, *refs):
    blocks, (top, mine, other, slopes, best, offset) = refs[:count], refs[count:]
    depth = states.shape[1]
    half = mine.shape[1]
    step = pl.program_id(0)

    @pl.when(step == 0)
    def _():
        row = 0
        for block in blocks:
            rows = block.shape[0]
            slopes[row : row + rows, :] = block[:, :depth]
            offset[row : row + rows, :] = block[:, depth:].astype(jnp.float32)
            row += rows
        best[...] = jnp.full(best.shape, -jnp.inf, jnp.float32)

    scores = lax.dot_general(
        slopes[...], states[...], (((1,), (1,)), ((), ())), preferred_element_type=jnp.float32
    )
    lifted = scores - old[...]
    most = best[...]
    for lane in range(0, tile, LANES):
        most = jnp.maximum(most, lifted[:, lane : lane + LANES])
    best[...] = most
    wide = offset[...]
    valued = jnp.concatenate(
        [scores[:, lane : lane + LANES] + wide for lane in range(0, tile, LANES)], axis=1
    )
    top[...] = jnp.maximum(prev[...], jnp.max(valued, axis=0, keepdims=True))

    @pl.when(step == tiles - 1)
    def _():
        lift = jnp.max((best[...] + offset[...]).T, axis=0, keepdims=True)
        mine[...] = lift[:, :half]
        other[...] = lift[:, half:]


def score(blocks, old, prev, states, tile=1024):
    count, depth = states.shape
    cuts = sum(block.shape[0] for block in blocks)
    tiles = count // tile
    whole = lambda shape: pl.BlockSpec(shape, lambda i: (0, 0))
    along = pl.BlockSpec((1, tile), lambda i: (0, i))
    lift = jax.ShapeDtypeStruct((1, cuts // 2), jnp.float32)
    return pl.pallas_call(
        functools.partial(score_body, tile, tiles, len(blocks)),
        grid=(tiles,),
        in_specs=[along, along, pl.BlockSpec((tile, depth), lambda i: (i, 0))]
        + [whole(block.shape) for block in blocks],
        out_specs=[along, whole(lift.shape), whole(lift.shape)],
        out_shape=[jax.ShapeDtypeStruct((1, count), jnp.float32), lift, lift],
        scratch_shapes=[
            pltpu.VMEM((cuts, depth), jnp.bfloat16),
            pltpu.VMEM((cuts, LANES), jnp.float32),
            pltpu.VMEM((cuts, LANES), jnp.float32),
        ],
        compiler_params=pltpu.CompilerParams(vmem_limit_bytes=24 << 20),
        cost_estimate=pl.CostEstimate(
            flops=2 * cuts * depth * count, bytes_accessed=2 * (count + cuts) * depth, transcendentals=0
        ),
    )(old, prev, states, *blocks)


def body(coefficients, intercepts, states, old_values):
    old = old_values[None, :]
    cuts = coefficients.shape[0]
    fence = lax.optimization_barrier

    own = pack(coefficients, intercepts)
    near = send(own, toward)
    peer = send(own, over_core)
    top, own_mine, own_other = score([own, peer], old, old, states)
    near, own, top = fence((near, own, top))
    two = send(near, toward)
    next_ = send(own, against)
    top, near_mine, near_other = score([near, send(near, over_core)], old, top, states)

    mine = jnp.concatenate([own_mine, near_mine], axis=0)
    other = jnp.concatenate([own_other, near_other], axis=0)
    lifts = jnp.maximum(mine, send(other, over_core))
    held = jnp.maximum(lifts[0:1], send(lifts[1:2], against))
    next_, two, top, held = fence((next_, two, top, held))
    blocks = [next_, two, send(next_, over_core), send(two, over_core)]
    top, mine, other = score(blocks, old, top, states)

    swapped = send(other, over_core)
    for_x = [send(top, over_x(d)) for d in (1, 2, 3)]
    swapped, for_x[0] = fence((swapped, for_x[0]))
    lifts = jnp.concatenate([held, jnp.maximum(mine, swapped)], axis=1)
    for_y = [send(lifts, over_y(d)) for d in (1, 2, 3)]
    top = functools.reduce(jnp.maximum, for_x, top)
    for_y[0], top = fence((for_y[0], top))
    lifts = functools.reduce(jnp.maximum, for_y, lifts)
    across = send(top, far)
    for_z = [send(lifts[:, cuts : 2 * cuts], toward), send(lifts[:, 2 * cuts :], two_back)]
    across, *for_z = fence((across, *for_z))
    new_values = jnp.maximum(top, across)
    cut_gaps = functools.reduce(jnp.maximum, for_z, lifts[:, :cuts])
    return new_values[0], cut_gaps[0]


def solution(mesh):
    placed = (P(("grp", "cut"), None), P(("grp", "cut")), P(("grp", "st"), None), P(("grp", "st")))
    return jax.shard_map(
        body,
        mesh=mesh,
        in_specs=placed,
        out_specs=(P(("grp", "st")), P(("grp", "cut"))),
        check_vma=False,
    )
```

```python
import functools

import jax
import jax.numpy as jnp
from jax import lax
from jax.experimental import pallas as pl
from jax.experimental.pallas import tpu as pltpu
from jax.sharding import PartitionSpec as P

AXES = ("grp", "cut", "st")
NX, NY, NZ, NC = 4, 4, 8, 2
LANES = 128
PACK_FLOPS = 10**10
PACK_VMEM = 24 << 20


def position(x, y, z, c):
    z_hi, z_lo = divmod(z % NZ, 4)
    return (((z_lo * NC + c % NC) * 8) + z_hi * NX + x % NX) * NY + y % NY


def routes(move):
    pairs = []
    for x in range(NX):
        for y in range(NY):
            for z in range(NZ):
                for c in range(NC):
                    pairs.append((position(x, y, z, c), position(*move(x, y, z, c))))
    return pairs


def send(block, move):
    return lax.ppermute(block, AXES, routes(move))


def over_core(x, y, z, c):
    return x, y, z, 1 - c


def toward(x, y, z, c):
    return x, y, z - 1 if c == 0 else z + 1, c


def against(x, y, z, c):
    return x, y, z + 1 if c == 0 else z - 1, c


def two_back(x, y, z, c):
    return x, y, z + 2 if c == 0 else z - 2, c


def far(x, y, z, c):
    return x, y, z + 4, c


def over_x(d):
    return lambda x, y, z, c: (x ^ d, y, z, c)


def over_y(d):
    return lambda x, y, z, c: (x, y ^ d, z, c)


def pack_body(coefficients, intercepts, own, slopes, row, arrived):
    depth = coefficients.shape[1]
    copies = [
        pltpu.make_async_copy(coefficients, slopes, arrived.at[0]),
        pltpu.make_async_copy(intercepts, row, arrived.at[1]),
    ]
    for copy in copies:
        copy.start()
    for copy in copies:
        copy.wait()
    own[:, :depth] = slopes[...]
    wide = jnp.broadcast_to(row[...].astype(jnp.float32), (LANES, row.shape[1])).T
    own[:, depth:] = wide.astype(jnp.bfloat16)


def pack(coefficients, intercepts):
    cuts, depth = coefficients.shape
    there = pl.BlockSpec(memory_space=pl.ANY)
    return pl.pallas_call(
        pack_body,
        in_specs=[there, there],
        out_specs=pl.BlockSpec(memory_space=pltpu.VMEM),
        out_shape=jax.ShapeDtypeStruct((cuts, depth + LANES), jnp.bfloat16),
        scratch_shapes=[
            pltpu.VMEM((cuts, depth), jnp.bfloat16),
            pltpu.VMEM((1, cuts), jnp.bfloat16),
            pltpu.SemaphoreType.DMA((2,)),
        ],
        compiler_params=pltpu.CompilerParams(vmem_limit_bytes=PACK_VMEM),
        cost_estimate=pl.CostEstimate(flops=PACK_FLOPS, bytes_accessed=4 * cuts * depth, transcendentals=0),
    )(coefficients, intercepts[None, :])


def score_body(tile, tiles, count, old, prev, states, *refs):
    blocks, (top, mine, other, slopes, best, offset) = refs[:count], refs[count:]
    depth = states.shape[1]
    half = mine.shape[1]
    step = pl.program_id(0)

    @pl.when(step == 0)
    def _():
        row = 0
        for block in blocks:
            rows = block.shape[0]
            slopes[row : row + rows, :] = block[:, :depth]
            offset[row : row + rows, :] = block[:, depth:].astype(jnp.float32)
            row += rows
        best[...] = jnp.full(best.shape, -jnp.inf, jnp.float32)

    scores = lax.dot_general(
        slopes[...], states[...], (((1,), (1,)), ((), ())), preferred_element_type=jnp.float32
    )
    lifted = scores - old[...]
    most = best[...]
    for lane in range(0, tile, LANES):
        most = jnp.maximum(most, lifted[:, lane : lane + LANES])
    best[...] = most
    wide = offset[...]
    valued = jnp.concatenate(
        [scores[:, lane : lane + LANES] + wide for lane in range(0, tile, LANES)], axis=1
    )
    top[...] = jnp.maximum(prev[...], jnp.max(valued, axis=0, keepdims=True))

    @pl.when(step == tiles - 1)
    def _():
        lift = jnp.max((best[...] + offset[...]).T, axis=0, keepdims=True)
        mine[...] = lift[:, :half]
        other[...] = lift[:, half:]


def score(blocks, old, prev, states, tile=1024):
    count, depth = states.shape
    cuts = sum(block.shape[0] for block in blocks)
    tiles = count // tile
    whole = lambda shape: pl.BlockSpec(shape, lambda i: (0, 0))
    along = pl.BlockSpec((1, tile), lambda i: (0, i))
    lift = jax.ShapeDtypeStruct((1, cuts // 2), jnp.float32)
    return pl.pallas_call(
        functools.partial(score_body, tile, tiles, len(blocks)),
        grid=(tiles,),
        in_specs=[along, along, pl.BlockSpec((tile, depth), lambda i: (i, 0))]
        + [whole(block.shape) for block in blocks],
        out_specs=[along, whole(lift.shape), whole(lift.shape)],
        out_shape=[jax.ShapeDtypeStruct((1, count), jnp.float32), lift, lift],
        scratch_shapes=[
            pltpu.VMEM((cuts, depth), jnp.bfloat16),
            pltpu.VMEM((cuts, LANES), jnp.float32),
            pltpu.VMEM((cuts, LANES), jnp.float32),
        ],
        compiler_params=pltpu.CompilerParams(vmem_limit_bytes=24 << 20),
        cost_estimate=pl.CostEstimate(
            flops=2 * cuts * depth * count, bytes_accessed=2 * (count + cuts) * depth, transcendentals=0
        ),
    )(old, prev, states, *blocks)


def body(coefficients, intercepts, states, old_values):
    old = old_values[None, :]
    cuts = coefficients.shape[0]
    fence = lax.optimization_barrier

    own = pack(coefficients, intercepts)
    near = send(own, toward)
    next_ = send(own, against)
    peer = send(own, over_core)
    top, own_mine, own_other = score([own, peer], old, old, states)
    near, next_, top = fence((near, next_, top))
    two = send(near, toward)
    blocks = [near, next_, send(near, over_core), send(next_, over_core)]
    top, side_mine, side_other = score(blocks, old, top, states)
    two, top = fence((two, top))
    top, two_mine, two_other = score([two, send(two, over_core)], old, top, states)

    mine = jnp.concatenate([own_mine, side_mine, two_mine], axis=1)
    swapped = send(jnp.concatenate([own_other, side_other, two_other], axis=1), over_core)
    for_x = [send(top, over_x(d)) for d in (1, 2, 3)]
    swapped, for_x[0] = fence((swapped, for_x[0]))
    lifts = jnp.maximum(mine, swapped)
    for_y = [send(lifts, over_y(d)) for d in (1, 2, 3)]
    top = functools.reduce(jnp.maximum, for_x, top)
    for_y[0], top = fence((for_y[0], top))
    lifts = functools.reduce(jnp.maximum, for_y, lifts)
    across = send(top, far)
    split = [lifts[:, k * cuts : (k + 1) * cuts] for k in range(4)]
    for_z = [send(split[1], against), send(split[2], toward), send(split[3], two_back)]
    across, *for_z = fence((across, *for_z))
    new_values = jnp.maximum(top, across)
    cut_gaps = functools.reduce(jnp.maximum, for_z, split[0])
    return new_values[0], cut_gaps[0]


def solution(mesh):
    placed = (P(("grp", "cut"), None), P(("grp", "cut")), P(("grp", "st"), None), P(("grp", "st")))
    return jax.shard_map(
        body,
        mesh=mesh,
        in_specs=placed,
        out_specs=(P(("grp", "st")), P(("grp", "cut"))),
        check_vma=False,
    )
```

```python
import functools

import jax
import jax.numpy as jnp
from jax import lax
from jax.experimental import pallas as pl
from jax.experimental.pallas import tpu as pltpu
from jax.sharding import PartitionSpec as P

AXES = ("grp", "cut", "st")
NX, NY, NZ, NC = 4, 4, 8, 2
LANES = 128
PACK_FLOPS = 10**10
PACK_VMEM = 24 << 20


def position(x, y, z, c):
    z_hi, z_lo = divmod(z % NZ, 4)
    return (((z_lo * NC + c % NC) * 8) + z_hi * NX + x % NX) * NY + y % NY


def routes(move):
    pairs = []
    for x in range(NX):
        for y in range(NY):
            for z in range(NZ):
                for c in range(NC):
                    pairs.append((position(x, y, z, c), position(*move(x, y, z, c))))
    return pairs


def send(block, move):
    return lax.ppermute(block, AXES, routes(move))


def over_core(x, y, z, c):
    return x, y, z, 1 - c


def toward(x, y, z, c):
    return x, y, z - 1 if c == 0 else z + 1, c


def against(x, y, z, c):
    return x, y, z + 1 if c == 0 else z - 1, c


def two_back(x, y, z, c):
    return x, y, z + 2 if c == 0 else z - 2, c


def far(x, y, z, c):
    return x, y, z + 4, c


def over_x(d):
    return lambda x, y, z, c: (x ^ d, y, z, c)


def over_y(d):
    return lambda x, y, z, c: (x, y ^ d, z, c)


def pack_body(coefficients, intercepts, own, slopes, row, arrived):
    depth = coefficients.shape[1]
    copies = [
        pltpu.make_async_copy(coefficients, slopes, arrived.at[0]),
        pltpu.make_async_copy(intercepts, row, arrived.at[1]),
    ]
    for copy in copies:
        copy.start()
    for copy in copies:
        copy.wait()
    own[:, :depth] = slopes[...]
    wide = jnp.broadcast_to(row[...].astype(jnp.float32), (LANES, row.shape[1])).T
    own[:, depth:] = wide.astype(jnp.bfloat16)


def pack(coefficients, intercepts):
    cuts, depth = coefficients.shape
    there = pl.BlockSpec(memory_space=pl.ANY)
    return pl.pallas_call(
        pack_body,
        in_specs=[there, there],
        out_specs=pl.BlockSpec(memory_space=pltpu.VMEM),
        out_shape=jax.ShapeDtypeStruct((cuts, depth + LANES), jnp.bfloat16),
        scratch_shapes=[
            pltpu.VMEM((cuts, depth), jnp.bfloat16),
            pltpu.VMEM((1, cuts), jnp.bfloat16),
            pltpu.SemaphoreType.DMA((2,)),
        ],
        compiler_params=pltpu.CompilerParams(vmem_limit_bytes=PACK_VMEM),
        cost_estimate=pl.CostEstimate(flops=PACK_FLOPS, bytes_accessed=4 * cuts * depth, transcendentals=0),
    )(coefficients, intercepts[None, :])


def score_body(tile, tiles, count, old, prev, states, *refs):
    blocks, (top, mine, other, slopes, best, offset) = refs[:count], refs[count:]
    depth = states.shape[1]
    half = mine.shape[1]
    step = pl.program_id(0)

    @pl.when(step == 0)
    def _():
        row = 0
        for block in blocks:
            rows = block.shape[0]
            slopes[row : row + rows, :] = block[:, :depth]
            offset[row : row + rows, :] = block[:, depth:].astype(jnp.float32)
            row += rows
        best[...] = jnp.full(best.shape, -jnp.inf, jnp.float32)

    scores = lax.dot_general(
        slopes[...], states[...], (((1,), (1,)), ((), ())), preferred_element_type=jnp.float32
    )
    lifted = scores - old[...]
    most = best[...]
    for lane in range(0, tile, LANES):
        most = jnp.maximum(most, lifted[:, lane : lane + LANES])
    best[...] = most
    wide = offset[...]
    valued = jnp.concatenate(
        [scores[:, lane : lane + LANES] + wide for lane in range(0, tile, LANES)], axis=1
    )
    top[...] = jnp.maximum(prev[...], jnp.max(valued, axis=0, keepdims=True))

    @pl.when(step == tiles - 1)
    def _():
        lift = jnp.max((best[...] + offset[...]).T, axis=0, keepdims=True)
        mine[...] = lift[:, :half]
        other[...] = lift[:, half:]


def score(blocks, old, prev, states, tile=1024):
    count, depth = states.shape
    cuts = sum(block.shape[0] for block in blocks)
    tiles = count // tile
    whole = lambda shape: pl.BlockSpec(shape, lambda i: (0, 0))
    along = pl.BlockSpec((1, tile), lambda i: (0, i))
    lift = jax.ShapeDtypeStruct((1, cuts // 2), jnp.float32)
    return pl.pallas_call(
        functools.partial(score_body, tile, tiles, len(blocks)),
        grid=(tiles,),
        in_specs=[along, along, pl.BlockSpec((tile, depth), lambda i: (i, 0))]
        + [whole(block.shape) for block in blocks],
        out_specs=[along, whole(lift.shape), whole(lift.shape)],
        out_shape=[jax.ShapeDtypeStruct((1, count), jnp.float32), lift, lift],
        scratch_shapes=[
            pltpu.VMEM((cuts, depth), jnp.bfloat16),
            pltpu.VMEM((cuts, LANES), jnp.float32),
            pltpu.VMEM((cuts, LANES), jnp.float32),
        ],
        compiler_params=pltpu.CompilerParams(vmem_limit_bytes=24 << 20),
        cost_estimate=pl.CostEstimate(
            flops=2 * cuts * depth * count, bytes_accessed=2 * (count + cuts) * depth, transcendentals=0
        ),
    )(old, prev, states, *blocks)


def body(coefficients, intercepts, states, old_values):
    old = old_values[None, :]
    cuts = coefficients.shape[0]
    fence = lax.optimization_barrier

    own = pack(coefficients, intercepts)
    near = send(own, toward)
    next_ = send(own, against)
    peer = send(own, over_core)
    top, own_mine, own_other = score([own, peer], old, old, states)
    near, next_, top = fence((near, next_, top))
    two = send(near, toward)
    blocks = [near, next_, send(near, over_core), send(next_, over_core)]
    top, side_mine, side_other = score(blocks, old, top, states)

    mine = jnp.concatenate([own_mine, side_mine], axis=1)
    lifts = jnp.maximum(mine, send(jnp.concatenate([own_other, side_other], axis=1), over_core))
    two, top, lifts = fence((two, top, lifts))
    split = [lifts[:, k * cuts : (k + 1) * cuts] for k in range(3)]
    back = [send(split[1], against), send(split[2], toward)]
    top, two_mine, two_other = score([two, send(two, over_core)], old, top, states)

    swapped = send(two_other, over_core)
    for_x = [send(top, over_x(d)) for d in (1, 2, 3)]
    swapped, for_x[0] = fence((swapped, for_x[0]))
    held = functools.reduce(jnp.maximum, back, split[0])
    lifts = jnp.concatenate([held, jnp.maximum(two_mine, swapped)], axis=1)
    for_y = [send(lifts, over_y(d)) for d in (1, 2, 3)]
    top = functools.reduce(jnp.maximum, for_x, top)
    for_y[0], top = fence((for_y[0], top))
    lifts = functools.reduce(jnp.maximum, for_y, lifts)
    across = send(top, far)
    returned = send(lifts[:, cuts:], two_back)
    across, returned = fence((across, returned))
    new_values = jnp.maximum(top, across)
    cut_gaps = jnp.maximum(returned, lifts[:, :cuts])
    return new_values[0], cut_gaps[0]


def solution(mesh):
    placed = (P(("grp", "cut"), None), P(("grp", "cut")), P(("grp", "st"), None), P(("grp", "st")))
    return jax.shard_map(
        body,
        mesh=mesh,
        in_specs=placed,
        out_specs=(P(("grp", "st")), P(("grp", "cut"))),
        check_vma=False,
    )
```

```python
import functools

import jax
import jax.numpy as jnp
from jax import lax
from jax.experimental import pallas as pl
from jax.experimental.pallas import tpu as pltpu
from jax.sharding import PartitionSpec as P

AXES = ("grp", "cut", "st")
NX, NY, NZ, NC = 4, 4, 8, 2
LANES = 128
PACK_FLOPS = 10**10
PACK_VMEM = 24 << 20


def position(x, y, z, c):
    z_hi, z_lo = divmod(z % NZ, 4)
    return (((z_lo * NC + c % NC) * 8) + z_hi * NX + x % NX) * NY + y % NY


def routes(move):
    pairs = []
    for x in range(NX):
        for y in range(NY):
            for z in range(NZ):
                for c in range(NC):
                    pairs.append((position(x, y, z, c), position(*move(x, y, z, c))))
    return pairs


def send(block, move):
    return lax.ppermute(block, AXES, routes(move))


def over_core(x, y, z, c):
    return x, y, z, 1 - c


def toward(x, y, z, c):
    return x, y, z - 1 if c == 0 else z + 1, c


def against(x, y, z, c):
    return x, y, z + 1 if c == 0 else z - 1, c


def two_back(x, y, z, c):
    return x, y, z + 2 if c == 0 else z - 2, c


def far(x, y, z, c):
    return x, y, z + 4, c


def over_x(d):
    return lambda x, y, z, c: (x ^ d, y, z, c)


def over_y(d):
    return lambda x, y, z, c: (x, y ^ d, z, c)


def pack_body(coefficients, intercepts, own, slopes, row, arrived):
    depth = coefficients.shape[1]
    copies = [
        pltpu.make_async_copy(coefficients, slopes, arrived.at[0]),
        pltpu.make_async_copy(intercepts, row, arrived.at[1]),
    ]
    for copy in copies:
        copy.start()
    for copy in copies:
        copy.wait()
    own[:, :depth] = slopes[...]
    wide = jnp.broadcast_to(row[...].astype(jnp.float32), (LANES, row.shape[1])).T
    own[:, depth:] = wide.astype(jnp.bfloat16)


def pack(coefficients, intercepts):
    cuts, depth = coefficients.shape
    there = pl.BlockSpec(memory_space=pl.ANY)
    return pl.pallas_call(
        pack_body,
        in_specs=[there, there],
        out_specs=pl.BlockSpec(memory_space=pltpu.VMEM),
        out_shape=jax.ShapeDtypeStruct((cuts, depth + LANES), jnp.bfloat16),
        scratch_shapes=[
            pltpu.VMEM((cuts, depth), jnp.bfloat16),
            pltpu.VMEM((1, cuts), jnp.bfloat16),
            pltpu.SemaphoreType.DMA((2,)),
        ],
        compiler_params=pltpu.CompilerParams(vmem_limit_bytes=PACK_VMEM),
        cost_estimate=pl.CostEstimate(flops=PACK_FLOPS, bytes_accessed=4 * cuts * depth, transcendentals=0),
    )(coefficients, intercepts[None, :])


def score_body(tile, tiles, count, old, prev, states, *refs):
    blocks, (top, mine, other, slopes, best, offset) = refs[:count], refs[count:]
    depth = states.shape[1]
    half = mine.shape[1]
    step = pl.program_id(0)

    @pl.when(step == 0)
    def _():
        row = 0
        for block in blocks:
            rows = block.shape[0]
            slopes[row : row + rows, :] = block[:, :depth]
            offset[row : row + rows, :] = block[:, depth:].astype(jnp.float32)
            row += rows
        best[...] = jnp.full(best.shape, -jnp.inf, jnp.float32)

    scores = lax.dot_general(
        slopes[...], states[...], (((1,), (1,)), ((), ())), preferred_element_type=jnp.float32
    )
    lifted = scores - old[...]
    most = best[...]
    for lane in range(0, tile, LANES):
        most = jnp.maximum(most, lifted[:, lane : lane + LANES])
    best[...] = most
    wide = offset[...]
    valued = jnp.concatenate(
        [scores[:, lane : lane + LANES] + wide for lane in range(0, tile, LANES)], axis=1
    )
    top[...] = jnp.maximum(prev[...], jnp.max(valued, axis=0, keepdims=True))

    @pl.when(step == tiles - 1)
    def _():
        lift = jnp.max((best[...] + offset[...]).T, axis=0, keepdims=True)
        mine[...] = lift[:, :half]
        other[...] = lift[:, half:]


def score(blocks, old, prev, states, tile=1024):
    count, depth = states.shape
    cuts = sum(block.shape[0] for block in blocks)
    tiles = count // tile
    whole = lambda shape: pl.BlockSpec(shape, lambda i: (0, 0))
    along = pl.BlockSpec((1, tile), lambda i: (0, i))
    lift = jax.ShapeDtypeStruct((1, cuts // 2), jnp.float32)
    return pl.pallas_call(
        functools.partial(score_body, tile, tiles, len(blocks)),
        grid=(tiles,),
        in_specs=[along, along, pl.BlockSpec((tile, depth), lambda i: (i, 0))]
        + [whole(block.shape) for block in blocks],
        out_specs=[along, whole(lift.shape), whole(lift.shape)],
        out_shape=[jax.ShapeDtypeStruct((1, count), jnp.float32), lift, lift],
        scratch_shapes=[
            pltpu.VMEM((cuts, depth), jnp.bfloat16),
            pltpu.VMEM((cuts, LANES), jnp.float32),
            pltpu.VMEM((cuts, LANES), jnp.float32),
        ],
        compiler_params=pltpu.CompilerParams(vmem_limit_bytes=24 << 20),
        cost_estimate=pl.CostEstimate(
            flops=2 * cuts * depth * count, bytes_accessed=2 * (count + cuts) * depth, transcendentals=0
        ),
    )(old, prev, states, *blocks)


def body(coefficients, intercepts, states, old_values):
    old = old_values[None, :]
    cuts = coefficients.shape[0]
    fence = lax.optimization_barrier

    own = pack(coefficients, intercepts)
    near = send(own, toward)
    next_ = send(own, against)
    peer = send(own, over_core)
    top, own_mine, own_other = score([own, peer], old, old, states)
    near, next_, top = fence((near, next_, top))
    two = send(near, toward)
    blocks = [near, next_, send(near, over_core), send(next_, over_core)]
    top, side_mine, side_other = score(blocks, old, top, states)

    mine = jnp.concatenate([own_mine, side_mine], axis=1)
    lifts = jnp.maximum(mine, send(jnp.concatenate([own_other, side_other], axis=1), over_core))
    two, top, lifts = fence((two, top, lifts))
    split = [lifts[:, k * cuts : (k + 1) * cuts] for k in range(3)]
    back = [send(split[1], against), send(split[2], toward)]
    top, two_mine, two_other = score([two, send(two, over_core)], old, top, states)

    swapped = send(two_other, over_core)
    for_x = [send(top, over_x(d)) for d in (1, 2, 3)]
    swapped, for_x[0] = fence((swapped, for_x[0]))
    held = functools.reduce(jnp.maximum, back, split[0])
    lifts = jnp.concatenate([held, jnp.maximum(two_mine, swapped)], axis=1)
    for_y = [send(lifts, over_y(d)) for d in (1, 2, 3)]
    top = functools.reduce(jnp.maximum, for_x, top)
    lifts = functools.reduce(jnp.maximum, for_y, lifts)
    across = send(top, far)
    returned = send(lifts[:, cuts:], two_back)
    across, returned = fence((across, returned))
    new_values = jnp.maximum(top, across)
    cut_gaps = jnp.maximum(returned, lifts[:, :cuts])
    return new_values[0], cut_gaps[0]


def solution(mesh):
    placed = (P(("grp", "cut"), None), P(("grp", "cut")), P(("grp", "st"), None), P(("grp", "st")))
    return jax.shard_map(
        body,
        mesh=mesh,
        in_specs=placed,
        out_specs=(P(("grp", "st")), P(("grp", "cut"))),
        check_vma=False,
    )
```

```python
import functools

import jax
import jax.numpy as jnp
from jax import lax
from jax.experimental import pallas as pl
from jax.experimental.pallas import tpu as pltpu
from jax.sharding import PartitionSpec as P

AXES = ("grp", "cut", "st")
NX, NY, NZ, NC = 4, 4, 8, 2
LANES = 128
PACK_FLOPS = 10**10
PACK_VMEM = 24 << 20


def position(x, y, z, c):
    z_hi, z_lo = divmod(z % NZ, 4)
    return (((z_lo * NC + c % NC) * 8) + z_hi * NX + x % NX) * NY + y % NY


def routes(move):
    pairs = []
    for x in range(NX):
        for y in range(NY):
            for z in range(NZ):
                for c in range(NC):
                    pairs.append((position(x, y, z, c), position(*move(x, y, z, c))))
    return pairs


def send(block, move):
    return lax.ppermute(block, AXES, routes(move))


def over_core(x, y, z, c):
    return x, y, z, 1 - c


def toward(x, y, z, c):
    return x, y, z - 1 if c == 0 else z + 1, c


def against(x, y, z, c):
    return x, y, z + 1 if c == 0 else z - 1, c


def two_back(x, y, z, c):
    return x, y, z + 2 if c == 0 else z - 2, c


def far(x, y, z, c):
    return x, y, z + 4, c


def over_x(d):
    return lambda x, y, z, c: (x ^ d, y, z, c)


def over_y(d):
    return lambda x, y, z, c: (x, y ^ d, z, c)


def pack_body(coefficients, intercepts, own, slopes, row, arrived):
    depth = coefficients.shape[1]
    copies = [
        pltpu.make_async_copy(coefficients, slopes, arrived.at[0]),
        pltpu.make_async_copy(intercepts, row, arrived.at[1]),
    ]
    for copy in copies:
        copy.start()
    for copy in copies:
        copy.wait()
    own[:, :depth] = slopes[...]
    wide = jnp.broadcast_to(row[...].astype(jnp.float32), (LANES, row.shape[1])).T
    own[:, depth:] = wide.astype(jnp.bfloat16)


def pack(coefficients, intercepts):
    cuts, depth = coefficients.shape
    there = pl.BlockSpec(memory_space=pl.ANY)
    return pl.pallas_call(
        pack_body,
        in_specs=[there, there],
        out_specs=pl.BlockSpec(memory_space=pltpu.VMEM),
        out_shape=jax.ShapeDtypeStruct((cuts, depth + LANES), jnp.bfloat16),
        scratch_shapes=[
            pltpu.VMEM((cuts, depth), jnp.bfloat16),
            pltpu.VMEM((1, cuts), jnp.bfloat16),
            pltpu.SemaphoreType.DMA((2,)),
        ],
        compiler_params=pltpu.CompilerParams(vmem_limit_bytes=PACK_VMEM),
        cost_estimate=pl.CostEstimate(flops=PACK_FLOPS, bytes_accessed=4 * cuts * depth, transcendentals=0),
    )(coefficients, intercepts[None, :])


def score_body(tile, tiles, count, old, prev, states, *refs):
    blocks, (top, mine, other, slopes, best, offset) = refs[:count], refs[count:]
    depth = states.shape[1]
    half = mine.shape[1]
    step = pl.program_id(0)

    @pl.when(step == 0)
    def _():
        row = 0
        for block in blocks:
            rows = block.shape[0]
            slopes[row : row + rows, :] = block[:, :depth]
            offset[row : row + rows, :] = block[:, depth:].astype(jnp.float32)
            row += rows
        best[...] = jnp.full(best.shape, -jnp.inf, jnp.float32)

    scores = lax.dot_general(
        slopes[...], states[...], (((1,), (1,)), ((), ())), preferred_element_type=jnp.float32
    )
    lifted = scores - old[...]
    most = best[...]
    for lane in range(0, tile, LANES):
        most = jnp.maximum(most, lifted[:, lane : lane + LANES])
    best[...] = most
    wide = offset[...]
    valued = jnp.concatenate(
        [scores[:, lane : lane + LANES] + wide for lane in range(0, tile, LANES)], axis=1
    )
    top[...] = jnp.maximum(prev[...], jnp.max(valued, axis=0, keepdims=True))

    @pl.when(step == tiles - 1)
    def _():
        lift = jnp.max((best[...] + offset[...]).T, axis=0, keepdims=True)
        mine[...] = lift[:, :half]
        other[...] = lift[:, half:]


def score(blocks, old, prev, states, tile=1024):
    count, depth = states.shape
    cuts = sum(block.shape[0] for block in blocks)
    tiles = count // tile
    whole = lambda shape: pl.BlockSpec(shape, lambda i: (0, 0))
    along = pl.BlockSpec((1, tile), lambda i: (0, i))
    lift = jax.ShapeDtypeStruct((1, cuts // 2), jnp.float32)
    return pl.pallas_call(
        functools.partial(score_body, tile, tiles, len(blocks)),
        grid=(tiles,),
        in_specs=[along, along, pl.BlockSpec((tile, depth), lambda i: (i, 0))]
        + [whole(block.shape) for block in blocks],
        out_specs=[along, whole(lift.shape), whole(lift.shape)],
        out_shape=[jax.ShapeDtypeStruct((1, count), jnp.float32), lift, lift],
        scratch_shapes=[
            pltpu.VMEM((cuts, depth), jnp.bfloat16),
            pltpu.VMEM((cuts, LANES), jnp.float32),
            pltpu.VMEM((cuts, LANES), jnp.float32),
        ],
        compiler_params=pltpu.CompilerParams(vmem_limit_bytes=24 << 20),
        cost_estimate=pl.CostEstimate(
            flops=2 * cuts * depth * count, bytes_accessed=2 * (count + cuts) * depth, transcendentals=0
        ),
    )(old, prev, states, *blocks)


def body(coefficients, intercepts, states, old_values):
    old = old_values[None, :]
    cuts = coefficients.shape[0]
    fence = lax.optimization_barrier

    own = pack(coefficients, intercepts)
    near = send(own, toward)
    next_ = send(own, against)
    peer = send(own, over_core)
    top, own_mine, own_other = score([own, peer], old, old, states)
    near, next_, top = fence((near, next_, top))
    two = send(near, toward)
    blocks = [near, next_, send(near, over_core), send(next_, over_core)]
    top, side_mine, side_other = score(blocks, old, top, states)

    mine = jnp.concatenate([own_mine, side_mine], axis=1)
    lifts = jnp.maximum(mine, send(jnp.concatenate([own_other, side_other], axis=1), over_core))
    two, top, lifts = fence((two, top, lifts))
    split = [lifts[:, k * cuts : (k + 1) * cuts] for k in range(3)]
    back = [send(split[1], against), send(split[2], toward)]
    top, two_mine, two_other = score([two, send(two, over_core)], old, top, states)

    swapped = send(two_other, over_core)
    for_x = [send(top, over_x(d)) for d in (1, 2, 3)]
    swapped, for_x[0] = fence((swapped, for_x[0]))
    returned = send(jnp.maximum(two_mine, swapped), two_back)
    held = functools.reduce(jnp.maximum, back, split[0])
    top = functools.reduce(jnp.maximum, for_x, top)
    across = send(top, far)
    lifts = jnp.maximum(held, returned)
    for_y = [send(lifts, over_y(d)) for d in (1, 2, 3)]
    across, *for_y = fence((across, *for_y))
    new_values = jnp.maximum(top, across)
    cut_gaps = functools.reduce(jnp.maximum, for_y, lifts)
    return new_values[0], cut_gaps[0]


def solution(mesh):
    placed = (P(("grp", "cut"), None), P(("grp", "cut")), P(("grp", "st"), None), P(("grp", "st")))
    return jax.shard_map(
        body,
        mesh=mesh,
        in_specs=placed,
        out_specs=(P(("grp", "st")), P(("grp", "cut"))),
        check_vma=False,
    )
```

```python
import functools

import jax
import jax.numpy as jnp
from jax import lax
from jax.experimental import pallas as pl
from jax.experimental.pallas import tpu as pltpu
from jax.sharding import PartitionSpec as P

AXES = ("grp", "cut", "st")
NX, NY, NZ, NC = 4, 4, 8, 2
LANES = 128
PACK_FLOPS = 10**10
PACK_VMEM = 55 << 20


def position(x, y, z, c):
    z_hi, z_lo = divmod(z % NZ, 4)
    return (((z_lo * NC + c % NC) * 8) + z_hi * NX + x % NX) * NY + y % NY


def routes(move):
    pairs = []
    for x in range(NX):
        for y in range(NY):
            for z in range(NZ):
                for c in range(NC):
                    pairs.append((position(x, y, z, c), position(*move(x, y, z, c))))
    return pairs


def send(block, move):
    return lax.ppermute(block, AXES, routes(move))


def over_core(x, y, z, c):
    return x, y, z, 1 - c


def toward(x, y, z, c):
    return x, y, z - 1 if c == 0 else z + 1, c


def against(x, y, z, c):
    return x, y, z + 1 if c == 0 else z - 1, c


def two_back(x, y, z, c):
    return x, y, z + 2 if c == 0 else z - 2, c


def far(x, y, z, c):
    return x, y, z + 4, c


def over_x(d):
    return lambda x, y, z, c: (x ^ d, y, z, c)


def over_y(d):
    return lambda x, y, z, c: (x, y ^ d, z, c)


def pack_body(coefficients, intercepts, own, slopes, row, arrived):
    depth = coefficients.shape[1]
    copies = [
        pltpu.make_async_copy(coefficients, slopes, arrived.at[0]),
        pltpu.make_async_copy(intercepts, row, arrived.at[1]),
    ]
    for copy in copies:
        copy.start()
    for copy in copies:
        copy.wait()
    own[:, :depth] = slopes[...]
    wide = jnp.broadcast_to(row[...].astype(jnp.float32), (LANES, row.shape[1])).T
    own[:, depth:] = wide.astype(jnp.bfloat16)


def pack(coefficients, intercepts):
    cuts, depth = coefficients.shape
    there = pl.BlockSpec(memory_space=pl.ANY)
    return pl.pallas_call(
        pack_body,
        in_specs=[there, there],
        out_specs=pl.BlockSpec(memory_space=pltpu.VMEM),
        out_shape=jax.ShapeDtypeStruct((cuts, depth + LANES), jnp.bfloat16),
        scratch_shapes=[
            pltpu.VMEM((cuts, depth), jnp.bfloat16),
            pltpu.VMEM((1, cuts), jnp.bfloat16),
            pltpu.SemaphoreType.DMA((2,)),
        ],
        compiler_params=pltpu.CompilerParams(vmem_limit_bytes=PACK_VMEM),
        cost_estimate=pl.CostEstimate(flops=PACK_FLOPS, bytes_accessed=4 * cuts * depth, transcendentals=0),
    )(coefficients, intercepts[None, :])


def score_body(tile, tiles, count, old, prev, states, *refs):
    blocks, (top, mine, other, slopes, best, offset) = refs[:count], refs[count:]
    depth = states.shape[1]
    half = mine.shape[1]
    step = pl.program_id(0)

    @pl.when(step == 0)
    def _():
        row = 0
        for block in blocks:
            rows = block.shape[0]
            slopes[row : row + rows, :] = block[:, :depth]
            offset[row : row + rows, :] = block[:, depth:].astype(jnp.float32)
            row += rows
        best[...] = jnp.full(best.shape, -jnp.inf, jnp.float32)

    scores = lax.dot_general(
        slopes[...], states[...], (((1,), (1,)), ((), ())), preferred_element_type=jnp.float32
    )
    lifted = scores - old[...]
    most = best[...]
    for lane in range(0, tile, LANES):
        most = jnp.maximum(most, lifted[:, lane : lane + LANES])
    best[...] = most
    wide = offset[...]
    valued = jnp.concatenate(
        [scores[:, lane : lane + LANES] + wide for lane in range(0, tile, LANES)], axis=1
    )
    top[...] = jnp.maximum(prev[...], jnp.max(valued, axis=0, keepdims=True))

    @pl.when(step == tiles - 1)
    def _():
        lift = jnp.max((best[...] + offset[...]).T, axis=0, keepdims=True)
        mine[...] = lift[:, :half]
        other[...] = lift[:, half:]


def score(blocks, old, prev, states, tile=1024):
    count, depth = states.shape
    cuts = sum(block.shape[0] for block in blocks)
    tiles = count // tile
    whole = lambda shape: pl.BlockSpec(shape, lambda i: (0, 0))
    along = pl.BlockSpec((1, tile), lambda i: (0, i))
    lift = jax.ShapeDtypeStruct((1, cuts // 2), jnp.float32)
    return pl.pallas_call(
        functools.partial(score_body, tile, tiles, len(blocks)),
        grid=(tiles,),
        in_specs=[along, along, pl.BlockSpec((tile, depth), lambda i: (i, 0))]
        + [whole(block.shape) for block in blocks],
        out_specs=[along, whole(lift.shape), whole(lift.shape)],
        out_shape=[jax.ShapeDtypeStruct((1, count), jnp.float32), lift, lift],
        scratch_shapes=[
            pltpu.VMEM((cuts, depth), jnp.bfloat16),
            pltpu.VMEM((cuts, LANES), jnp.float32),
            pltpu.VMEM((cuts, LANES), jnp.float32),
        ],
        compiler_params=pltpu.CompilerParams(vmem_limit_bytes=24 << 20),
        cost_estimate=pl.CostEstimate(
            flops=2 * cuts * depth * count, bytes_accessed=2 * (count + cuts) * depth, transcendentals=0
        ),
    )(old, prev, states, *blocks)


def body(coefficients, intercepts, states, old_values):
    old = old_values[None, :]
    cuts = coefficients.shape[0]
    fence = lax.optimization_barrier

    own = pack(coefficients, intercepts)
    near = send(own, toward)
    next_ = send(own, against)
    peer = send(own, over_core)
    top, own_mine, own_other = score([own, peer], old, old, states)
    near, next_, top = fence((near, next_, top))
    two = send(near, toward)
    blocks = [near, next_, send(near, over_core), send(next_, over_core)]
    top, side_mine, side_other = score(blocks, old, top, states)

    mine = jnp.concatenate([own_mine, side_mine], axis=1)
    lifts = jnp.maximum(mine, send(jnp.concatenate([own_other, side_other], axis=1), over_core))
    two, top, lifts = fence((two, top, lifts))
    split = [lifts[:, k * cuts : (k + 1) * cuts] for k in range(3)]
    back = [send(split[1], against), send(split[2], toward)]
    top, two_mine, two_other = score([two, send(two, over_core)], old, top, states)

    swapped = send(two_other, over_core)
    for_x = [send(top, over_x(d)) for d in (1, 2, 3)]
    swapped, for_x[0] = fence((swapped, for_x[0]))
    held = functools.reduce(jnp.maximum, back, split[0])
    lifts = jnp.concatenate([held, jnp.maximum(two_mine, swapped)], axis=1)
    for_y = [send(lifts, over_y(d)) for d in (1, 2, 3)]
    top = functools.reduce(jnp.maximum, for_x, top)
    lifts = functools.reduce(jnp.maximum, for_y, lifts)
    across = send(top, far)
    returned = send(lifts[:, cuts:], two_back)
    new_values = jnp.maximum(top, across)
    new_values, returned = fence((new_values, returned))
    cut_gaps = jnp.maximum(returned, lifts[:, :cuts])
    return new_values[0], cut_gaps[0]


def solution(mesh):
    placed = (P(("grp", "cut"), None), P(("grp", "cut")), P(("grp", "st"), None), P(("grp", "st")))
    return jax.shard_map(
        body,
        mesh=mesh,
        in_specs=placed,
        out_specs=(P(("grp", "st")), P(("grp", "cut"))),
        check_vma=False,
    )
```

```python
import functools

import jax
import jax.numpy as jnp
from jax import lax
from jax.experimental import pallas as pl
from jax.experimental.pallas import tpu as pltpu
from jax.sharding import PartitionSpec as P

AXES = ("grp", "cut", "st")
NX, NY, NZ, NC = 4, 4, 8, 2
LANES = 128
PACK_FLOPS = 10**7
PACK_VMEM = 56 << 20


def position(x, y, z, c):
    z_hi, z_lo = divmod(z % NZ, 4)
    return (((z_lo * NC + c % NC) * 8) + z_hi * NX + x % NX) * NY + y % NY


def routes(move):
    pairs = []
    for x in range(NX):
        for y in range(NY):
            for z in range(NZ):
                for c in range(NC):
                    pairs.append((position(x, y, z, c), position(*move(x, y, z, c))))
    return pairs


def send(block, move):
    return lax.ppermute(block, AXES, routes(move))


def over_core(x, y, z, c):
    return x, y, z, 1 - c


def toward(x, y, z, c):
    return x, y, z - 1 if c == 0 else z + 1, c


def against(x, y, z, c):
    return x, y, z + 1 if c == 0 else z - 1, c


def two_back(x, y, z, c):
    return x, y, z + 2 if c == 0 else z - 2, c


def far(x, y, z, c):
    return x, y, z + 4, c


def over_x(d):
    return lambda x, y, z, c: (x ^ d, y, z, c)


def over_y(d):
    return lambda x, y, z, c: (x, y ^ d, z, c)


def pack_body(coefficients, intercepts, own, slopes, row, arrived):
    depth = coefficients.shape[1]
    copies = [
        pltpu.make_async_copy(coefficients, slopes, arrived.at[0]),
        pltpu.make_async_copy(intercepts, row, arrived.at[1]),
    ]
    for copy in copies:
        copy.start()
    for copy in copies:
        copy.wait()
    own[:, :depth] = slopes[...]
    wide = jnp.broadcast_to(row[...].astype(jnp.float32), (LANES, row.shape[1])).T
    own[:, depth:] = wide.astype(jnp.bfloat16)


def pack(coefficients, intercepts):
    cuts, depth = coefficients.shape
    there = pl.BlockSpec(memory_space=pl.ANY)
    return pl.pallas_call(
        pack_body,
        in_specs=[there, there],
        out_specs=pl.BlockSpec(memory_space=pltpu.VMEM),
        out_shape=jax.ShapeDtypeStruct((cuts, depth + LANES), jnp.bfloat16),
        scratch_shapes=[
            pltpu.VMEM((cuts, depth), jnp.bfloat16),
            pltpu.VMEM((1, cuts), jnp.bfloat16),
            pltpu.SemaphoreType.DMA((2,)),
        ],
        compiler_params=pltpu.CompilerParams(vmem_limit_bytes=PACK_VMEM),
        cost_estimate=pl.CostEstimate(flops=PACK_FLOPS, bytes_accessed=4 * cuts * depth, transcendentals=0),
    )(coefficients, intercepts[None, :])


def score_body(tile, tiles, count, old, prev, states, *refs):
    blocks, (top, mine, other, slopes, best, offset) = refs[:count], refs[count:]
    depth = states.shape[1]
    half = mine.shape[1]
    step = pl.program_id(0)

    @pl.when(step == 0)
    def _():
        row = 0
        for block in blocks:
            rows = block.shape[0]
            slopes[row : row + rows, :] = block[:, :depth]
            offset[row : row + rows, :] = block[:, depth:].astype(jnp.float32)
            row += rows
        best[...] = jnp.full(best.shape, -jnp.inf, jnp.float32)

    scores = lax.dot_general(
        slopes[...], states[...], (((1,), (1,)), ((), ())), preferred_element_type=jnp.float32
    )
    lifted = scores - old[...]
    most = best[...]
    for lane in range(0, tile, LANES):
        most = jnp.maximum(most, lifted[:, lane : lane + LANES])
    best[...] = most
    wide = offset[...]
    valued = jnp.concatenate(
        [scores[:, lane : lane + LANES] + wide for lane in range(0, tile, LANES)], axis=1
    )
    top[...] = jnp.maximum(prev[...], jnp.max(valued, axis=0, keepdims=True))

    @pl.when(step == tiles - 1)
    def _():
        lift = jnp.max((best[...] + offset[...]).T, axis=0, keepdims=True)
        mine[...] = lift[:, :half]
        other[...] = lift[:, half:]


def score(blocks, old, prev, states, tile=1024):
    count, depth = states.shape
    cuts = sum(block.shape[0] for block in blocks)
    tiles = count // tile
    whole = lambda shape: pl.BlockSpec(shape, lambda i: (0, 0))
    along = pl.BlockSpec((1, tile), lambda i: (0, i))
    lift = jax.ShapeDtypeStruct((1, cuts // 2), jnp.float32)
    return pl.pallas_call(
        functools.partial(score_body, tile, tiles, len(blocks)),
        grid=(tiles,),
        in_specs=[along, along, pl.BlockSpec((tile, depth), lambda i: (i, 0))]
        + [whole(block.shape) for block in blocks],
        out_specs=[along, whole(lift.shape), whole(lift.shape)],
        out_shape=[jax.ShapeDtypeStruct((1, count), jnp.float32), lift, lift],
        scratch_shapes=[
            pltpu.VMEM((cuts, depth), jnp.bfloat16),
            pltpu.VMEM((cuts, LANES), jnp.float32),
            pltpu.VMEM((cuts, LANES), jnp.float32),
        ],
        compiler_params=pltpu.CompilerParams(vmem_limit_bytes=24 << 20),
        cost_estimate=pl.CostEstimate(
            flops=2 * cuts * depth * count, bytes_accessed=2 * (count + cuts) * depth, transcendentals=0
        ),
    )(old, prev, states, *blocks)


def body(coefficients, intercepts, states, old_values):
    old = old_values[None, :]
    cuts = coefficients.shape[0]
    fence = lax.optimization_barrier

    own = pack(coefficients, intercepts)
    near = send(own, toward)
    next_ = send(own, against)
    peer = send(own, over_core)
    top, own_mine, own_other = score([own, peer], old, old, states)
    near, next_, top = fence((near, next_, top))
    two = send(near, toward)
    blocks = [near, next_, send(near, over_core), send(next_, over_core)]
    top, side_mine, side_other = score(blocks, old, top, states)

    mine = jnp.concatenate([own_mine, side_mine], axis=1)
    lifts = jnp.maximum(mine, send(jnp.concatenate([own_other, side_other], axis=1), over_core))
    two, top, lifts = fence((two, top, lifts))
    split = [lifts[:, k * cuts : (k + 1) * cuts] for k in range(3)]
    back = [send(split[1], against), send(split[2], toward)]
    top, two_mine, two_other = score([two, send(two, over_core)], old, top, states)

    swapped = send(two_other, over_core)
    for_x = [send(top, over_x(d)) for d in (1, 2, 3)]
    swapped, for_x[0] = fence((swapped, for_x[0]))
    held = functools.reduce(jnp.maximum, back, split[0])
    lifts = jnp.concatenate([held, jnp.maximum(two_mine, swapped)], axis=1)
    for_y = [send(lifts, over_y(d)) for d in (1, 2, 3)]
    top = functools.reduce(jnp.maximum, for_x, top)
    lifts = functools.reduce(jnp.maximum, for_y, lifts)
    across = send(top, far)
    returned = send(lifts[:, cuts:], two_back)
    new_values = jnp.maximum(top, across)
    new_values, returned = fence((new_values, returned))
    cut_gaps = jnp.maximum(returned, lifts[:, :cuts])
    return new_values[0], cut_gaps[0]


def solution(mesh):
    placed = (P(("grp", "cut"), None), P(("grp", "cut")), P(("grp", "st"), None), P(("grp", "st")))
    return jax.shard_map(
        body,
        mesh=mesh,
        in_specs=placed,
        out_specs=(P(("grp", "st")), P(("grp", "cut"))),
        check_vma=False,
    )
```

```python
import functools

import jax
import jax.numpy as jnp
from jax import lax
from jax.experimental import pallas as pl
from jax.experimental.pallas import tpu as pltpu
from jax.sharding import PartitionSpec as P

AXES = ("grp", "cut", "st")
NX, NY, NZ, NC = 4, 4, 8, 2
LANES = 128
PACK_FLOPS = 10**10
PACK_VMEM = 24 << 20


def position(x, y, z, c):
    z_hi, z_lo = divmod(z % NZ, 4)
    return (((z_lo * NC + c % NC) * 8) + z_hi * NX + x % NX) * NY + y % NY


def routes(move):
    pairs = []
    for x in range(NX):
        for y in range(NY):
            for z in range(NZ):
                for c in range(NC):
                    pairs.append((position(x, y, z, c), position(*move(x, y, z, c))))
    return pairs


def send(block, move):
    return lax.ppermute(block, AXES, routes(move))


def over_core(x, y, z, c):
    return x, y, z, 1 - c


def toward(x, y, z, c):
    return x, y, z - 1 if c == 0 else z + 1, c


def against(x, y, z, c):
    return x, y, z + 1 if c == 0 else z - 1, c


def two_back(x, y, z, c):
    return x, y, z + 2 if c == 0 else z - 2, c


def far(x, y, z, c):
    return x, y, z + 4, c


def over_x(d):
    return lambda x, y, z, c: (x ^ d, y, z, c)


def over_y(d):
    return lambda x, y, z, c: (x, y ^ d, z, c)


def pack_body(coefficients, intercepts, own, slopes, row, arrived):
    depth = coefficients.shape[1]
    copies = [
        pltpu.make_async_copy(coefficients, slopes, arrived.at[0]),
        pltpu.make_async_copy(intercepts, row, arrived.at[1]),
    ]
    for copy in copies:
        copy.start()
    for copy in copies:
        copy.wait()
    own[:, :depth] = slopes[...]
    wide = jnp.broadcast_to(row[...].astype(jnp.float32), (LANES, row.shape[1])).T
    own[:, depth:] = wide.astype(jnp.bfloat16)


def pack(coefficients, intercepts):
    cuts, depth = coefficients.shape
    there = pl.BlockSpec(memory_space=pl.ANY)
    return pl.pallas_call(
        pack_body,
        in_specs=[there, there],
        out_specs=pl.BlockSpec(memory_space=pltpu.VMEM),
        out_shape=jax.ShapeDtypeStruct((cuts, depth + LANES), jnp.bfloat16),
        scratch_shapes=[
            pltpu.VMEM((cuts, depth), jnp.bfloat16),
            pltpu.VMEM((1, cuts), jnp.bfloat16),
            pltpu.SemaphoreType.DMA((2,)),
        ],
        compiler_params=pltpu.CompilerParams(vmem_limit_bytes=PACK_VMEM),
        cost_estimate=pl.CostEstimate(flops=PACK_FLOPS, bytes_accessed=4 * cuts * depth, transcendentals=0),
    )(coefficients, intercepts[None, :])


def score_body(tile, tiles, count, old, prev, states, *refs):
    blocks, (top, mine, other, slopes, best, offset) = refs[:count], refs[count:]
    depth = states.shape[1]
    half = mine.shape[1]
    step = pl.program_id(0)

    @pl.when(step == 0)
    def _():
        row = 0
        for block in blocks:
            rows = block.shape[0]
            slopes[row : row + rows, :] = block[:, :depth]
            offset[row : row + rows, :] = block[:, depth:].astype(jnp.float32)
            row += rows
        best[...] = jnp.full(best.shape, -jnp.inf, jnp.float32)

    scores = lax.dot_general(
        slopes[...], states[...], (((1,), (1,)), ((), ())), preferred_element_type=jnp.float32
    )
    lifted = scores - old[...]
    most = best[...]
    for lane in range(0, tile, LANES):
        most = jnp.maximum(most, lifted[:, lane : lane + LANES])
    best[...] = most
    wide = offset[...]
    valued = jnp.concatenate(
        [scores[:, lane : lane + LANES] + wide for lane in range(0, tile, LANES)], axis=1
    )
    top[...] = jnp.maximum(prev[...], jnp.max(valued, axis=0, keepdims=True))

    @pl.when(step == tiles - 1)
    def _():
        lift = jnp.max((best[...] + offset[...]).T, axis=0, keepdims=True)
        mine[...] = lift[:, :half]
        other[...] = lift[:, half:]


def score(blocks, old, prev, states, tile=1024):
    count, depth = states.shape
    cuts = sum(block.shape[0] for block in blocks)
    tiles = count // tile
    whole = lambda shape: pl.BlockSpec(shape, lambda i: (0, 0))
    along = pl.BlockSpec((1, tile), lambda i: (0, i))
    lift = jax.ShapeDtypeStruct((1, cuts // 2), jnp.float32)
    return pl.pallas_call(
        functools.partial(score_body, tile, tiles, len(blocks)),
        grid=(tiles,),
        in_specs=[along, along, pl.BlockSpec((tile, depth), lambda i: (i, 0))]
        + [whole(block.shape) for block in blocks],
        out_specs=[along, whole(lift.shape), whole(lift.shape)],
        out_shape=[jax.ShapeDtypeStruct((1, count), jnp.float32), lift, lift],
        scratch_shapes=[
            pltpu.VMEM((cuts, depth), jnp.bfloat16),
            pltpu.VMEM((cuts, LANES), jnp.float32),
            pltpu.VMEM((cuts, LANES), jnp.float32),
        ],
        compiler_params=pltpu.CompilerParams(vmem_limit_bytes=24 << 20),
        cost_estimate=pl.CostEstimate(
            flops=2 * cuts * depth * count, bytes_accessed=2 * (count + cuts) * depth, transcendentals=0
        ),
    )(old, prev, states, *blocks)


def body(coefficients, intercepts, states, old_values):
    old = old_values[None, :]
    cuts = coefficients.shape[0]
    fence = lax.optimization_barrier

    own = pack(coefficients, intercepts)
    near = send(own, toward)
    next_ = send(own, against)
    peer = send(own, over_core)
    top, own_mine, own_other = score([own, peer], old, old, states)
    near, next_, top = fence((near, next_, top))
    two = send(near, toward)
    blocks = [near, next_, send(near, over_core), send(next_, over_core)]
    top, side_mine, side_other = score(blocks, old, top, states)

    mine = jnp.concatenate([own_mine, side_mine], axis=1)
    lifts = jnp.maximum(mine, send(jnp.concatenate([own_other, side_other], axis=1), over_core))
    two, top, lifts = fence((two, top, lifts))
    split = [lifts[:, k * cuts : (k + 1) * cuts] for k in range(3)]
    back = [send(split[1], against), send(split[2], toward)]
    top, two_mine, two_other = score([two, send(two, over_core)], old, top, states)

    swapped = send(two_other, over_core)
    held = functools.reduce(jnp.maximum, back, split[0])
    top = jnp.maximum(top, send(top, over_x(1)))
    swapped, top = fence((swapped, top))
    lifts = jnp.concatenate([held, jnp.maximum(two_mine, swapped)], axis=1)
    lifts = jnp.maximum(lifts, send(lifts, over_y(1)))
    top_two = send(top, over_x(2))
    lifts, top_two = fence((lifts, top_two))
    top = jnp.maximum(top, top_two)
    lifts = jnp.maximum(lifts, send(lifts, over_y(2)))
    across = send(top, far)
    returned = send(lifts[:, cuts:], two_back)
    new_values = jnp.maximum(top, across)
    cut_gaps = jnp.maximum(returned, lifts[:, :cuts])
    return new_values[0], cut_gaps[0]


def solution(mesh):
    placed = (P(("grp", "cut"), None), P(("grp", "cut")), P(("grp", "st"), None), P(("grp", "st")))
    return jax.shard_map(
        body,
        mesh=mesh,
        in_specs=placed,
        out_specs=(P(("grp", "st")), P(("grp", "cut"))),
        check_vma=False,
    )
```

```python
import functools

import jax
import jax.numpy as jnp
from jax import lax
from jax.experimental import pallas as pl
from jax.experimental.pallas import tpu as pltpu
from jax.sharding import PartitionSpec as P

AXES = ("grp", "cut", "st")
NX, NY, NZ, NC = 4, 4, 8, 2
LANES = 128
PACK_FLOPS = 10**10
PACK_VMEM = 24 << 20


def position(x, y, z, c):
    z_hi, z_lo = divmod(z % NZ, 4)
    return (((z_lo * NC + c % NC) * 8) + z_hi * NX + x % NX) * NY + y % NY


def routes(move):
    pairs = []
    for x in range(NX):
        for y in range(NY):
            for z in range(NZ):
                for c in range(NC):
                    pairs.append((position(x, y, z, c), position(*move(x, y, z, c))))
    return pairs


def send(block, move):
    return lax.ppermute(block, AXES, routes(move))


def over_core(x, y, z, c):
    return x, y, z, 1 - c


def toward(x, y, z, c):
    return x, y, z - 1 if c == 0 else z + 1, c


def against(x, y, z, c):
    return x, y, z + 1 if c == 0 else z - 1, c


def two_back(x, y, z, c):
    return x, y, z + 2 if c == 0 else z - 2, c


def far(x, y, z, c):
    return x, y, z + 4, c


def over_x(d):
    return lambda x, y, z, c: (x ^ d, y, z, c)


def over_y(d):
    return lambda x, y, z, c: (x, y ^ d, z, c)


def pack_body(coefficients, intercepts, own, slopes, row, arrived):
    depth = coefficients.shape[1]
    copies = [
        pltpu.make_async_copy(coefficients, slopes, arrived.at[0]),
        pltpu.make_async_copy(intercepts, row, arrived.at[1]),
    ]
    for copy in copies:
        copy.start()
    for copy in copies:
        copy.wait()
    own[:, :depth] = slopes[...]
    wide = jnp.broadcast_to(row[...].astype(jnp.float32), (LANES, row.shape[1])).T
    own[:, depth:] = wide.astype(jnp.bfloat16)


def pack(coefficients, intercepts):
    cuts, depth = coefficients.shape
    there = pl.BlockSpec(memory_space=pl.ANY)
    return pl.pallas_call(
        pack_body,
        in_specs=[there, there],
        out_specs=pl.BlockSpec(memory_space=pltpu.VMEM),
        out_shape=jax.ShapeDtypeStruct((cuts, depth + LANES), jnp.bfloat16),
        scratch_shapes=[
            pltpu.VMEM((cuts, depth), jnp.bfloat16),
            pltpu.VMEM((1, cuts), jnp.bfloat16),
            pltpu.SemaphoreType.DMA((2,)),
        ],
        compiler_params=pltpu.CompilerParams(vmem_limit_bytes=PACK_VMEM),
        cost_estimate=pl.CostEstimate(flops=PACK_FLOPS, bytes_accessed=4 * cuts * depth, transcendentals=0),
    )(coefficients, intercepts[None, :])


def score_body(tile, tiles, count, old, prev, states, *refs):
    blocks, (top, mine, other, slopes, best, offset) = refs[:count], refs[count:]
    depth = states.shape[1]
    half = mine.shape[1]
    step = pl.program_id(0)

    @pl.when(step == 0)
    def _():
        row = 0
        for block in blocks:
            rows = block.shape[0]
            slopes[row : row + rows, :] = block[:, :depth]
            offset[row : row + rows, :] = block[:, depth:].astype(jnp.float32)
            row += rows
        best[...] = jnp.full(best.shape, -jnp.inf, jnp.float32)

    scores = lax.dot_general(
        slopes[...], states[...], (((1,), (1,)), ((), ())), preferred_element_type=jnp.float32
    )
    lifted = scores - old[...]
    most = best[...]
    for lane in range(0, tile, LANES):
        most = jnp.maximum(most, lifted[:, lane : lane + LANES])
    best[...] = most
    wide = offset[...]
    valued = jnp.concatenate(
        [scores[:, lane : lane + LANES] + wide for lane in range(0, tile, LANES)], axis=1
    )
    top[...] = jnp.maximum(prev[...], jnp.max(valued, axis=0, keepdims=True))

    @pl.when(step == tiles - 1)
    def _():
        lift = jnp.max((best[...] + offset[...]).T, axis=0, keepdims=True)
        mine[...] = lift[:, :half]
        other[...] = lift[:, half:]


def score(blocks, old, prev, states, tile=1024):
    count, depth = states.shape
    cuts = sum(block.shape[0] for block in blocks)
    tiles = count // tile
    whole = lambda shape: pl.BlockSpec(shape, lambda i: (0, 0))
    along = pl.BlockSpec((1, tile), lambda i: (0, i))
    lift = jax.ShapeDtypeStruct((1, cuts // 2), jnp.float32)
    return pl.pallas_call(
        functools.partial(score_body, tile, tiles, len(blocks)),
        grid=(tiles,),
        in_specs=[along, along, pl.BlockSpec((tile, depth), lambda i: (i, 0))]
        + [whole(block.shape) for block in blocks],
        out_specs=[along, whole(lift.shape), whole(lift.shape)],
        out_shape=[jax.ShapeDtypeStruct((1, count), jnp.float32), lift, lift],
        scratch_shapes=[
            pltpu.VMEM((cuts, depth), jnp.bfloat16),
            pltpu.VMEM((cuts, LANES), jnp.float32),
            pltpu.VMEM((cuts, LANES), jnp.float32),
        ],
        compiler_params=pltpu.CompilerParams(vmem_limit_bytes=24 << 20),
        cost_estimate=pl.CostEstimate(
            flops=2 * cuts * depth * count, bytes_accessed=2 * (count + cuts) * depth, transcendentals=0
        ),
    )(old, prev, states, *blocks)


def body(coefficients, intercepts, states, old_values):
    old = old_values[None, :]
    cuts = coefficients.shape[0]
    fence = lax.optimization_barrier

    own = pack(coefficients, intercepts)
    near = send(own, toward)
    next_ = send(own, against)
    peer = send(own, over_core)
    top, own_mine, own_other = score([own, peer], old, old, states)
    near, next_, top = fence((near, next_, top))
    two = send(near, toward)
    blocks = [near, next_, send(near, over_core), send(next_, over_core)]
    top, side_mine, side_other = score(blocks, old, top, states)

    mine = jnp.concatenate([own_mine, side_mine], axis=1)
    lifts = jnp.maximum(mine, send(jnp.concatenate([own_other, side_other], axis=1), over_core))
    two, top, lifts = fence((two, top, lifts))
    split = [lifts[:, k * cuts : (k + 1) * cuts] for k in range(3)]
    back = [send(split[1], against), send(split[2], toward)]
    top, two_mine, two_other = score([two, send(two, over_core)], old, top, states)

    swapped = send(two_other, over_core)
    for_x = [send(top, over_x(d)) for d in (1, 2, 3)]
    swapped, for_x[0] = fence((swapped, for_x[0]))
    held = functools.reduce(jnp.maximum, back, split[0])
    lifts = jnp.concatenate([held, jnp.maximum(two_mine, swapped)], axis=1)
    for_y = [send(lifts, over_y(d)) for d in (1, 2, 3)]
    top = functools.reduce(jnp.maximum, for_x, top)
    lifts = functools.reduce(jnp.maximum, for_y, lifts)
    across = send(top, far)
    returned = send(lifts[:, cuts:], two_back)
    new_values = jnp.maximum(top, across)
    new_values, returned = fence((new_values, returned))
    cut_gaps = jnp.maximum(returned, lifts[:, :cuts])
    return new_values[0], cut_gaps[0]


def solution(mesh):
    placed = (P(("grp", "cut"), None), P(("grp", "cut")), P(("grp", "st"), None), P(("grp", "st")))
    return jax.shard_map(
        body,
        mesh=mesh,
        in_specs=placed,
        out_specs=(P(("grp", "st")), P(("grp", "cut"))),
        check_vma=False,
    )
```

```python
import functools

import jax
import jax.numpy as jnp
from jax import lax
from jax.experimental import pallas as pl
from jax.experimental.pallas import tpu as pltpu
from jax.sharding import PartitionSpec as P

AXES = ("grp", "cut", "st")
NX, NY, NZ, NC = 4, 4, 8, 2
LANES = 128
PACK_FLOPS = 10**10
PACK_VMEM = 24 << 20


def position(x, y, z, c):
    z_hi, z_lo = divmod(z % NZ, 4)
    return (((z_lo * NC + c % NC) * 8) + z_hi * NX + x % NX) * NY + y % NY


def routes(move):
    pairs = []
    for x in range(NX):
        for y in range(NY):
            for z in range(NZ):
                for c in range(NC):
                    pairs.append((position(x, y, z, c), position(*move(x, y, z, c))))
    return pairs


def send(block, move):
    return lax.ppermute(block, AXES, routes(move))


def over_core(x, y, z, c):
    return x, y, z, 1 - c


def toward(x, y, z, c):
    return x, y, z - 1 if c == 0 else z + 1, c


def against(x, y, z, c):
    return x, y, z + 1 if c == 0 else z - 1, c


def two_back(x, y, z, c):
    return x, y, z + 2 if c == 0 else z - 2, c


def far(x, y, z, c):
    return x, y, z + 4, c


def over_x(d):
    return lambda x, y, z, c: (x ^ d, y, z, c)


def over_y(d):
    return lambda x, y, z, c: (x, y ^ d, z, c)


def pack_body(coefficients, intercepts, own, slopes, row, arrived):
    depth = coefficients.shape[1]
    copies = [
        pltpu.make_async_copy(coefficients, slopes, arrived.at[0]),
        pltpu.make_async_copy(intercepts, row, arrived.at[1]),
    ]
    for copy in copies:
        copy.start()
    for copy in copies:
        copy.wait()
    own[:, :depth] = slopes[...]
    wide = jnp.broadcast_to(row[...].astype(jnp.float32), (LANES, row.shape[1])).T
    own[:, depth:] = wide.astype(jnp.bfloat16)


def pack(coefficients, intercepts):
    cuts, depth = coefficients.shape
    there = pl.BlockSpec(memory_space=pl.ANY)
    return pl.pallas_call(
        pack_body,
        in_specs=[there, there],
        out_specs=pl.BlockSpec(memory_space=pltpu.VMEM),
        out_shape=jax.ShapeDtypeStruct((cuts, depth + LANES), jnp.bfloat16),
        scratch_shapes=[
            pltpu.VMEM((cuts, depth), jnp.bfloat16),
            pltpu.VMEM((1, cuts), jnp.bfloat16),
            pltpu.SemaphoreType.DMA((2,)),
        ],
        compiler_params=pltpu.CompilerParams(vmem_limit_bytes=PACK_VMEM),
        cost_estimate=pl.CostEstimate(flops=PACK_FLOPS, bytes_accessed=4 * cuts * depth, transcendentals=0),
    )(coefficients, intercepts[None, :])


def score_body(tile, tiles, count, old, prev, states, *refs):
    blocks, (top, mine, other, slopes, best, offset) = refs[:count], refs[count:]
    depth = states.shape[1]
    half = mine.shape[1]
    step = pl.program_id(0)

    @pl.when(step == 0)
    def _():
        row = 0
        for block in blocks:
            rows = block.shape[0]
            slopes[row : row + rows, :] = block[:, :depth]
            offset[row : row + rows, :] = block[:, depth:].astype(jnp.float32)
            row += rows
        best[...] = jnp.full(best.shape, -jnp.inf, jnp.float32)

    scores = lax.dot_general(
        slopes[...], states[...], (((1,), (1,)), ((), ())), preferred_element_type=jnp.float32
    )
    lifted = scores - old[...]
    most = best[...]
    for lane in range(0, tile, LANES):
        most = jnp.maximum(most, lifted[:, lane : lane + LANES])
    best[...] = most
    wide = offset[...]
    valued = jnp.concatenate(
        [scores[:, lane : lane + LANES] + wide for lane in range(0, tile, LANES)], axis=1
    )
    top[...] = jnp.maximum(prev[...], jnp.max(valued, axis=0, keepdims=True))

    @pl.when(step == tiles - 1)
    def _():
        lift = jnp.max((best[...] + offset[...]).T, axis=0, keepdims=True)
        mine[...] = lift[:, :half]
        other[...] = lift[:, half:]


def score(blocks, old, prev, states, tile=1024):
    count, depth = states.shape
    cuts = sum(block.shape[0] for block in blocks)
    tiles = count // tile
    whole = lambda shape: pl.BlockSpec(shape, lambda i: (0, 0))
    along = pl.BlockSpec((1, tile), lambda i: (0, i))
    lift = jax.ShapeDtypeStruct((1, cuts // 2), jnp.float32)
    return pl.pallas_call(
        functools.partial(score_body, tile, tiles, len(blocks)),
        grid=(tiles,),
        in_specs=[along, along, pl.BlockSpec((tile, depth), lambda i: (i, 0))]
        + [whole(block.shape) for block in blocks],
        out_specs=[along, whole(lift.shape), whole(lift.shape)],
        out_shape=[jax.ShapeDtypeStruct((1, count), jnp.float32), lift, lift],
        scratch_shapes=[
            pltpu.VMEM((cuts, depth), jnp.bfloat16),
            pltpu.VMEM((cuts, LANES), jnp.float32),
            pltpu.VMEM((cuts, LANES), jnp.float32),
        ],
        compiler_params=pltpu.CompilerParams(vmem_limit_bytes=24 << 20),
        cost_estimate=pl.CostEstimate(
            flops=2 * cuts * depth * count, bytes_accessed=2 * (count + cuts) * depth, transcendentals=0
        ),
    )(old, prev, states, *blocks)


def exchange(block):
    return [send(block, over_core)]


def body(coefficients, intercepts, states, old_values):
    old = old_values[None, :]
    cuts = coefficients.shape[0]
    fence = lax.optimization_barrier

    own = pack(coefficients, intercepts)
    near = send(own, toward)
    peer = send(own, over_core)
    next_ = send(peer, toward)
    top, own_mine, own_other = score([own, peer], old, old, states)
    near, next_, top = fence((near, next_, top))
    two = send(near, toward)
    blocks = [near, *exchange(next_), *exchange(near), next_]
    top, side_mine, side_other = score(blocks, old, top, states)

    mine = jnp.concatenate([own_mine, side_mine], axis=1)
    lifts = jnp.maximum(mine, send(jnp.concatenate([own_other, side_other], axis=1), over_core))
    two, top, lifts = fence((two, top, lifts))
    split = [lifts[:, k * cuts : (k + 1) * cuts] for k in range(3)]
    back = [send(split[1], against), send(split[2], toward)]
    top, two_mine, two_other = score([two, send(two, over_core)], old, top, states)

    swapped = send(two_other, over_core)
    for_x = [send(top, over_x(d)) for d in (1, 2, 3)]
    swapped, for_x[0] = fence((swapped, for_x[0]))
    held = functools.reduce(jnp.maximum, back, split[0])
    lifts = jnp.concatenate([held, jnp.maximum(two_mine, swapped)], axis=1)
    for_y = [send(lifts, over_y(d)) for d in (1, 2, 3)]
    top = functools.reduce(jnp.maximum, for_x, top)
    lifts = functools.reduce(jnp.maximum, for_y, lifts)
    across = send(top, far)
    returned = send(lifts[:, cuts:], two_back)
    new_values = jnp.maximum(top, across)
    new_values, returned = fence((new_values, returned))
    cut_gaps = jnp.maximum(returned, lifts[:, :cuts])
    return new_values[0], cut_gaps[0]


def solution(mesh):
    placed = (P(("grp", "cut"), None), P(("grp", "cut")), P(("grp", "st"), None), P(("grp", "st")))
    return jax.shard_map(
        body,
        mesh=mesh,
        in_specs=placed,
        out_specs=(P(("grp", "st")), P(("grp", "cut"))),
        check_vma=False,
    )
```

```python
import functools

import jax
import jax.numpy as jnp
from jax import lax
from jax.experimental import pallas as pl
from jax.experimental.pallas import tpu as pltpu
from jax.sharding import PartitionSpec as P

AXES = ("grp", "cut", "st")
NX, NY, NZ, NC = 4, 4, 8, 2
LANES = 128
PACK_FLOPS = 10**10
PACK_VMEM = 24 << 20


def position(x, y, z, c):
    z_hi, z_lo = divmod(z % NZ, 4)
    return (((z_lo * NC + c % NC) * 8) + z_hi * NX + x % NX) * NY + y % NY


def routes(move):
    pairs = []
    for x in range(NX):
        for y in range(NY):
            for z in range(NZ):
                for c in range(NC):
                    pairs.append((position(x, y, z, c), position(*move(x, y, z, c))))
    return pairs


def send(block, move):
    return lax.ppermute(block, AXES, routes(move))


def over_core(x, y, z, c):
    return x, y, z, 1 - c


def toward(x, y, z, c):
    return x, y, z - 1 if c == 0 else z + 1, c


def against(x, y, z, c):
    return x, y, z + 1 if c == 0 else z - 1, c


def two_back(x, y, z, c):
    return x, y, z + 2 if c == 0 else z - 2, c


def far(x, y, z, c):
    return x, y, z + 4, c


def over_x(d):
    return lambda x, y, z, c: (x ^ d, y, z, c)


def over_y(d):
    return lambda x, y, z, c: (x, y ^ d, z, c)


def pack_body(coefficients, intercepts, own, slopes, row, arrived):
    depth = coefficients.shape[1]
    copies = [
        pltpu.make_async_copy(coefficients, slopes, arrived.at[0]),
        pltpu.make_async_copy(intercepts, row, arrived.at[1]),
    ]
    for copy in copies:
        copy.start()
    for copy in copies:
        copy.wait()
    own[:, :depth] = slopes[...]
    wide = jnp.broadcast_to(row[...].astype(jnp.float32), (LANES, row.shape[1])).T
    own[:, depth:] = wide.astype(jnp.bfloat16)


def pack(coefficients, intercepts):
    cuts, depth = coefficients.shape
    there = pl.BlockSpec(memory_space=pl.ANY)
    return pl.pallas_call(
        pack_body,
        in_specs=[there, there],
        out_specs=pl.BlockSpec(memory_space=pltpu.VMEM),
        out_shape=jax.ShapeDtypeStruct((cuts, depth + LANES), jnp.bfloat16),
        scratch_shapes=[
            pltpu.VMEM((cuts, depth), jnp.bfloat16),
            pltpu.VMEM((1, cuts), jnp.bfloat16),
            pltpu.SemaphoreType.DMA((2,)),
        ],
        compiler_params=pltpu.CompilerParams(vmem_limit_bytes=PACK_VMEM),
        cost_estimate=pl.CostEstimate(flops=PACK_FLOPS, bytes_accessed=4 * cuts * depth, transcendentals=0),
    )(coefficients, intercepts[None, :])


def score_body(tile, tiles, count, old, prev, states, *refs):
    blocks, (top, mine, other, slopes, best, offset) = refs[:count], refs[count:]
    depth = states.shape[1]
    half = mine.shape[1]
    step = pl.program_id(0)

    @pl.when(step == 0)
    def _():
        row = 0
        for block in blocks:
            rows = block.shape[0]
            slopes[row : row + rows, :] = block[:, :depth]
            offset[row : row + rows, :] = block[:, depth:].astype(jnp.float32)
            row += rows
        best[...] = jnp.full(best.shape, -jnp.inf, jnp.float32)

    scores = lax.dot_general(
        slopes[...], states[...], (((1,), (1,)), ((), ())), preferred_element_type=jnp.float32
    )
    lifted = scores - old[...]
    most = best[...]
    for lane in range(0, tile, LANES):
        most = jnp.maximum(most, lifted[:, lane : lane + LANES])
    best[...] = most
    wide = offset[...]
    valued = jnp.concatenate(
        [scores[:, lane : lane + LANES] + wide for lane in range(0, tile, LANES)], axis=1
    )
    top[...] = jnp.maximum(prev[...], jnp.max(valued, axis=0, keepdims=True))

    @pl.when(step == tiles - 1)
    def _():
        lift = jnp.max((best[...] + offset[...]).T, axis=0, keepdims=True)
        mine[...] = lift[:, :half]
        other[...] = lift[:, half:]


def score(blocks, old, prev, states, tile=1024):
    count, depth = states.shape
    cuts = sum(block.shape[0] for block in blocks)
    tiles = count // tile
    whole = lambda shape: pl.BlockSpec(shape, lambda i: (0, 0))
    along = pl.BlockSpec((1, tile), lambda i: (0, i))
    lift = jax.ShapeDtypeStruct((1, cuts // 2), jnp.float32)
    return pl.pallas_call(
        functools.partial(score_body, tile, tiles, len(blocks)),
        grid=(tiles,),
        in_specs=[along, along, pl.BlockSpec((tile, depth), lambda i: (i, 0))]
        + [whole(block.shape) for block in blocks],
        out_specs=[along, whole(lift.shape), whole(lift.shape)],
        out_shape=[jax.ShapeDtypeStruct((1, count), jnp.float32), lift, lift],
        scratch_shapes=[
            pltpu.VMEM((cuts, depth), jnp.bfloat16),
            pltpu.VMEM((cuts, LANES), jnp.float32),
            pltpu.VMEM((cuts, LANES), jnp.float32),
        ],
        compiler_params=pltpu.CompilerParams(vmem_limit_bytes=24 << 20),
        cost_estimate=pl.CostEstimate(
            flops=2 * cuts * depth * count, bytes_accessed=2 * (count + cuts) * depth, transcendentals=0
        ),
    )(old, prev, states, *blocks)


def body(coefficients, intercepts, states, old_values):
    old = old_values[None, :]
    cuts = coefficients.shape[0]
    fence = lax.optimization_barrier

    own = pack(coefficients, intercepts)
    near = send(own, toward)
    next_ = send(own, against)
    peer = send(own, over_core)
    top, own_mine, own_other = score([own, peer], old, old, states)
    near, next_, top = fence((near, next_, top))
    two = send(near, toward)
    blocks = [near, next_, send(near, over_core), send(next_, over_core)]
    top, side_mine, side_other = score(blocks, old, top, states)

    mine = jnp.concatenate([own_mine, side_mine], axis=1)
    lifts = jnp.maximum(mine, send(jnp.concatenate([own_other, side_other], axis=1), over_core))
    two, top, lifts = fence((two, top, lifts))
    split = [lifts[:, k * cuts : (k + 1) * cuts] for k in range(3)]
    back = [send(split[1], against), send(split[2], toward)]
    top, two_mine, two_other = score([two, send(two, over_core)], old, top, states)

    swapped = send(two_other, over_core)
    for_x = [send(top, over_x(d)) for d in (1, 2, 3)]
    swapped, for_x[0] = fence((swapped, for_x[0]))
    held = functools.reduce(jnp.maximum, back, split[0])
    lifts = jnp.concatenate([held, jnp.maximum(two_mine, swapped)], axis=1)
    for_y = [send(lifts, over_y(d)) for d in (1, 2, 3)]
    top = functools.reduce(jnp.maximum, for_x, top)
    for_y[0], top = fence((for_y[0], top))
    lifts = functools.reduce(jnp.maximum, for_y, lifts)
    across = send(top, far)
    returned = send(lifts[:, cuts:], two_back)
    new_values = jnp.maximum(top, across)
    cut_gaps = jnp.maximum(returned, lifts[:, :cuts])
    return new_values[0], cut_gaps[0]


def solution(mesh):
    placed = (P(("grp", "cut"), None), P(("grp", "cut")), P(("grp", "st"), None), P(("grp", "st")))
    return jax.shard_map(
        body,
        mesh=mesh,
        in_specs=placed,
        out_specs=(P(("grp", "st")), P(("grp", "cut"))),
        check_vma=False,
    )
```
